256 devices in a mesh: row: 16 (over x, z_lo, core), col: 16 (over y, z_hi).
Axes of the slice: x: 4, y: 4, z: 8 (z_hi: 4, z_lo: 2; z = z_hi * 2 + z_lo), core: 2. Of those that a mesh axis runs over, the one named last changes fastest.
Arguments:
- features: bfloat16 [32768, 256], P(('row', 'col')), may hold values from -6 to 6
- degrees: int32 [32768], P(('row', 'col')), may hold values from 256 to 1023
- tile_values: bfloat16 [16, 16, 16, 8, 128, 128], P('row', 'col'), may hold values from 0 to 1
- tile_index: int32 [16, 16, 16, 8], P('row', 'col'), may hold values from 0 to 15, as said below
- tile_count: int32 [16, 16, 16], P('row', 'col'), may hold values from 1 to 8, as said below
- self_weight: bfloat16 [256, 256], replicated, may hold values from -0.375 to 0.375
- neigh_weight: bfloat16 [256, 256], replicated, may hold values from -1.5 to 1.5
- bias: float32 [256], replicated, may hold values from -3 to 3
- out_grad: bfloat16 [32768, 256], P(('row', 'col')), may hold values from -6 to 6
Outputs:
- output: bfloat16 [32768, 256], P(('row', 'col'))
- grad_features: bfloat16 [32768, 256], P(('row', 'col'))
- self_grad: float32 [256, 256], replicated
- neigh_grad: float32 [256, 256], replicated
- bias_grad: float32 [256], replicated
The draws below stay inside these ranges and needn't reach their ends.
Inputs may be any that keep to these rules, and one draw needn't show every extreme that they name: `tile_index`: within one grid block and column piece the 8 slots name distinct positions. `tile_count`: loads differ between grid blocks; in every draw some column piece has all 8 slots live.
All inputs are finite; a program needn't handle non-finite values.
Results may differ from the reference program's by a relative error of at most 0.012.
Values may be sent and summed in bfloat16 or wider, within the bound.
A program may use at most 128 MiB of HBM per device.

```python
import jax
import jax.numpy as jnp
from jax import lax

F = 256
TILE = 128
NP = 128
KP = 8
NODES = 32768
N_ROW = 16
N_COL = 16


def draw_tile_index(key, part):
    key = jax.random.fold_in(key, 11)
    tile_span = NP // TILE
    candidates = N_COL * tile_span * tile_span
    scores = jax.random.randint(key, (N_ROW, N_COL, N_ROW, candidates), 0, 1 << 30)
    ranking = jnp.argsort(scores, axis=-1, stable=True)
    return ranking[..., :KP].astype(jnp.int32)


def draw_tile_count(key, part):
    key = jax.random.fold_in(key, 23)
    level_key, count_key, spot_key = jax.random.split(key, 3)
    levels = jax.random.randint(level_key, (N_ROW, N_COL, 1), 1, 5)
    upper_bound = levels * (KP // 4) + 1
    counts = 1 + jax.random.randint(count_key, (N_ROW, N_COL, N_ROW), 0, upper_bound)
    counts = jnp.minimum(counts, KP)
    full_spot = jax.random.randint(spot_key, (), 0, N_ROW * N_COL * N_ROW)
    flat_index = jnp.arange(N_ROW * N_COL * N_ROW, dtype=jnp.int32).reshape(N_ROW, N_COL, N_ROW)
    return jnp.where(flat_index == full_spot, KP, counts).astype(jnp.int32)


def with_ends(drawn, rng, least, largest):
    longest = drawn.shape.index(max(drawn.shape))
    spots = []
    for shift in (0, 1):
        where = [jax.random.randint(jax.random.fold_in(rng, axis), (), 0, length) for axis, length in enumerate(drawn.shape)]
        where[longest] = (where[longest] + shift) % drawn.shape[longest]
        spots.append(tuple(where))
    return drawn.at[spots[0]].set(least).at[spots[1]].set(largest)


def steps_of(key, extent, cuts, least, largest):
    loudness = 1.0
    for position, blocks in cuts:
        draws = jax.random.uniform(jax.random.fold_in(jax.random.fold_in(key, 6), position), (blocks,), jnp.float32, least / len(cuts), largest / len(cuts))
        loudness = loudness * jnp.repeat(jnp.exp(draws), extent[position] // blocks).reshape((-1,) + (1,) * (len(extent) - 1 - position))
    return loudness


def bell_draw(own_key, extent, deviation, limit, cuts=(), held_as=jnp.bfloat16):
    result = deviation * jax.random.normal(own_key, extent, jnp.float32)
    if cuts:
        result = result * steps_of(own_key, extent, cuts, -0.22, 0.18)
    return jnp.clip(result, -limit, limit).astype(held_as)


def setup_inputs(seed: int = 0) -> dict:
    splits = jax.random.split(jax.random.key(seed), 10)
    features = bell_draw(splits[0], (NODES, F), 1.0, 6.0, ((0, 256),))
    degrees = with_ends(jax.random.randint(splits[1], (NODES,), 256, 1024), jax.random.fold_in(splits[1], 1), 256, 1023).astype(jnp.int32)
    tile_values = jnp.clip(1.0 * jax.random.uniform(splits[2], (N_ROW, N_COL, N_ROW, KP, TILE, TILE), jnp.float32) ** steps_of(splits[2], (N_ROW, N_COL, N_ROW, KP, TILE, TILE), ((0, 16), (1, 16)), -0.2, 0.2), 0.0, 1.0).astype(jnp.bfloat16)
    tile_index = draw_tile_index(jax.random.fold_in(splits[9], 71), 0)
    tile_count = draw_tile_count(jax.random.fold_in(splits[9], 71), 0)
    self_weight = bell_draw(splits[5], (F, F), F ** -0.5, 0.375)
    neigh_weight = bell_draw(splits[6], (F, F), (F // 16) ** -0.5, 1.5)
    bias = bell_draw(splits[7], (F,), 0.5, 3.0, (), jnp.float32)
    out_grad = bell_draw(splits[8], (NODES, F), 1.0, 6.0, ((0, 256),))
    return dict(features=features, degrees=degrees, tile_values=tile_values, tile_index=tile_index, tile_count=tile_count, self_weight=self_weight, neigh_weight=neigh_weight, bias=bias, out_grad=out_grad)


def gelu_tanh(value):
    return jax.nn.gelu(value, approximate=True)

def reference(features, degrees, tile_values, tile_index, tile_count, self_weight, neigh_weight, bias, out_grad):
    tile_span = NP // TILE
    rows_tiles = N_COL * NP // TILE
    blocks = features.reshape(N_ROW, N_COL, NP, F)
    slot_ids = jnp.arange(KP, dtype=jnp.int32)
    piece_ids = jnp.arange(N_ROW, dtype=jnp.int32)

    def forward_row(row_idx):

        def one_block(running, col_idx):
            tile_vals = tile_values[row_idx, col_idx].astype(jnp.float32)
            slot_index = tile_index[row_idx, col_idx]
            live_slots = (slot_ids[None, :] < tile_count[row_idx, col_idx][:, None]).astype(jnp.float32)
            tile_rows = slot_index // tile_span
            tile_cols = slot_index % tile_span
            source = blocks[:, col_idx].reshape(N_ROW, tile_span, TILE, F)
            picked = source[piece_ids[:, None], tile_cols].astype(jnp.float32)
            product = jnp.einsum('pkab,pkbf->pkaf', tile_vals, picked) * live_slots[:, :, None, None]
            summed = jax.ops.segment_sum(product.reshape(-1, TILE, F), tile_rows.reshape(-1), num_segments=rows_tiles)
            return (running + summed.reshape(N_COL * NP, F), None)
        total, _ = lax.scan(one_block, jnp.zeros((N_COL * NP, F), jnp.float32), jnp.arange(N_COL, dtype=jnp.int32))
        return total
    aggregate = lax.map(forward_row, jnp.arange(N_ROW, dtype=jnp.int32)).reshape(NODES, F)
    inverse = 1.0 / degrees.astype(jnp.float32)
    neighbour_mean = (aggregate * inverse[:, None]).astype(jnp.bfloat16)
    preact = jnp.dot(features, self_weight, preferred_element_type=jnp.float32)
    preact = preact + jnp.dot(neighbour_mean, neigh_weight, preferred_element_type=jnp.float32) + bias.astype(jnp.float32)
    activated, grad_fn = jax.vjp(gelu_tanh, preact)
    output = activated.astype(jnp.bfloat16)
    grad_pre, = grad_fn(out_grad.astype(jnp.float32))
    grad_preact = grad_pre.astype(jnp.bfloat16)
    self_grad = jnp.dot(features.T, grad_preact, preferred_element_type=jnp.float32)
    neigh_grad = jnp.dot(neighbour_mean.T, grad_preact, preferred_element_type=jnp.float32)
    bias_grad = lax.optimization_barrier(jnp.sum(grad_preact.astype(jnp.float32), axis=0))
    scaled_grad = (jnp.dot(grad_preact, neigh_weight.T, preferred_element_type=jnp.float32) * inverse[:, None]).astype(jnp.bfloat16)
    grad_blocks = scaled_grad.reshape(N_ROW, N_COL * NP, F)

    def backward_block(running, block_idx):
        row_idx = block_idx // N_COL
        col_idx = block_idx % N_COL
        tile_vals = tile_values[row_idx, col_idx].astype(jnp.float32)
        slot_index = tile_index[row_idx, col_idx]
        live_slots = (slot_ids[None, :] < tile_count[row_idx, col_idx][:, None]).astype(jnp.float32)
        tile_rows = slot_index // tile_span
        tile_cols = slot_index % tile_span
        row_source = grad_blocks[row_idx].reshape(rows_tiles, TILE, F)
        picked = row_source[tile_rows].astype(jnp.float32)
        product = jnp.einsum('pkab,pkaf->pkbf', tile_vals, picked) * live_slots[:, :, None, None]
        seg_keys = piece_ids[:, None] * tile_span + tile_cols
        summed = jax.ops.segment_sum(product.reshape(-1, TILE, F), seg_keys.reshape(-1), num_segments=N_ROW * tile_span)
        running = running.at[:, col_idx].add(summed.reshape(N_ROW, NP, F))
        return (running, None)
    back_sum, _ = lax.scan(backward_block, jnp.zeros((N_ROW, N_COL, NP, F), jnp.float32), jnp.arange(N_ROW * N_COL, dtype=jnp.int32))
    back_sum = back_sum.reshape(NODES, F)
    grad_features = (jnp.dot(grad_preact, self_weight.T, preferred_element_type=jnp.float32) + back_sum).astype(jnp.bfloat16)
    return (output, grad_features, self_grad, neigh_grad, bias_grad)
```

```python
import functools

import jax
import jax.numpy as jnp
from jax import lax
from jax.experimental import pallas as pl
from jax.experimental.pallas import tpu as pltpu
from jax.sharding import PartitionSpec as P

MESH = pl.DeviceIdType.MESH
F32 = jnp.float32
BF16 = jnp.bfloat16
T = 128
W = 256
CHIPS = [(dx, dz) for dx in (2, 1, 3, 0) for dz in (1, 0) if dx or dz]
PLANE = [(dx, dy) for dx in range(4) for dy in range(4) if dx or dy]
FAR = (2, 1, 3)
GELU_C = 0.7978845608028654


def dot(lhs, rhs, lhs_dim=1, rhs_dim=0):
    return lax.dot_general(
        lhs, rhs, (((lhs_dim,), (rhs_dim,)), ((), ())), preferred_element_type=F32
    )


def device(x, zl, c, y, zh):
    return (x * 4 + zl * 2 + c, y * 4 + zh)


def split_rows(total):
    high = total.astype(BF16).astype(F32)
    return high, total - high


def bias_block(total):
    high, low = split_rows(total)
    line = lax.broadcasted_iota(jnp.int32, (16, W), 0)
    return jnp.where(line == 0, high, jnp.where(line == 1, low, 0.0)).astype(BF16)


def kernel(
    slot_s, feats_h, deg_h, tiles_h, ws_h, wn_h, bias_h, og_h,
    out_h, gf_h, sg_h, ng_h, bg_h,
    tiles, tiles_t, dense, dense_t, feats_all, grads_all, deg_v, ws, wn, bias_v, og_v,
    base, recip, part_b, recv_by, sum_z, recv_bz, gp_v, nm_v, out_v, gf_v, self_keep,
    part_d, recv_ds, sum_d, recv_d,
    ar1_s, ar1_r, ar2_s, ar2_r, ar3_s, ar3_r, ar4, ar5_r, sg_v, ng_v, bg_v,
    local_sem, a_ss, a_rs, af_ss, af_rs, by_ss, by_rs, bz_ss, bz_rs,
    cz_ss, cz_rs, cy_ss, cy_rs, ds_ss, ds_rs, d_ss, d_rs,
    r1_ss, r1_rs, r2_ss, r2_rs, r3_ss, r3_rs, r4_ss, r4_rs, r5_ss, r5_rs,
):
    a = lax.axis_index("row")
    b = lax.axis_index("col")
    x, zl, c = a // 4, (a // 2) % 2, a % 2
    y, zh = b // 4, b % 4
    z = zh * 2 + zl
    sib = device(x, zl, 1 - c, y, zh)
    sent = []

    def send(src, dst, send_sem, recv_sem, where):
        copy = pltpu.make_async_remote_copy(
            src_ref=src, dst_ref=dst, send_sem=send_sem, recv_sem=recv_sem,
            device_id=where, device_id_type=MESH,
        )
        copy.start()
        sent.append(copy)
        return copy

    def chip(dx, dz):
        return (x + dx) % 4, (zl + dz) % 2

    loads = [
        pltpu.make_async_copy(feats_h, feats_all.at[a], local_sem.at[0]),
        pltpu.make_async_copy(tiles_h, tiles, local_sem.at[1]),
        pltpu.make_async_copy(ws_h, ws, local_sem.at[2]),
        pltpu.make_async_copy(wn_h, wn, local_sem.at[3]),
        pltpu.make_async_copy(bias_h, bias_v, local_sem.at[4]),
        pltpu.make_async_copy(og_h, og_v, local_sem.at[5]),
        pltpu.make_async_copy(deg_h, deg_v, local_sem.at[6]),
    ]
    for load in loads:
        load.start()

    partners = [sib]
    partners += [device(*chip(dx, dz), c, y, zh) for dx, dz in CHIPS]
    partners += [device((x + dx) % 4, zl, c, (y + dy) % 4, zh) for dx, dy in PLANE if dy]
    partners += [
        device(x, zz % 2, c, y, zz // 2)
        for zz in [(z + d) % 8 for d in range(1, 8)]
    ]
    barrier = pltpu.get_barrier_semaphore()
    for partner in partners:
        pl.semaphore_signal(barrier, inc=1, device_id=partner, device_id_type=MESH)
    pl.semaphore_wait(barrier, len(partners))

    own_to_sib = send(feats_h, feats_all.at[a], a_ss.at[7], a_rs.at[7], sib)
    a_sent = []
    for j, (dx, dz) in enumerate(CHIPS):
        where = device(*chip(dx, dz), c, y, zh)
        a_sent.append(send(feats_h, feats_all.at[a], a_ss.at[j], a_rs.at[j], where))

    for load in loads:
        load.wait()

    def build(q, carry):
        r = (q % 4) * 4 + q // 4
        for p in range(16):
            slot = slot_s[p, r]
            tile = tiles[p * 8 + jnp.minimum(slot, 7)]
            dense[q, :, p * T : (p + 1) * T] = jnp.where(slot < 8, tile, jnp.zeros_like(tile))
        return carry

    lax.fori_loop(0, 16, build, 0)
    base[...] = dot(feats_all[a], ws[...]) + bias_v[...]
    inverse = jnp.broadcast_to(1.0 / deg_v[...].astype(F32), (T, T)).T
    recip[...] = jnp.concatenate([inverse, inverse], axis=1)

    forwards = []
    for j in (4, 1, 3, 5, 6, 0, 2):
        dx, dz = CHIPS[j]
        a_sent[j].wait_recv()
        px, pz = chip(-dx, dz)
        piece = px * 4 + pz * 2 + c
        forwards.append(
            send(feats_all.at[piece], feats_all.at[piece], af_ss.at[j], af_rs.at[j], sib)
        )
    own_to_sib.wait_recv()
    for copy in forwards:
        copy.wait_recv()

    gathered = feats_all[...].reshape(16 * T, W)
    by_sent = []
    for i, dz in enumerate((2, 1, 3, 0)):
        zz = (zh + dz) % 4
        part = dot(dense[pl.ds(zz * 4, 4)].reshape(4 * T, 16 * T), gathered)
        part_b[i] = part.reshape(4, T, W).astype(BF16)
        row = []
        for k, dy in enumerate(FAR):
            yy = (y + dy) % 4
            row.append(
                send(
                    part_b.at[i, yy], recv_by.at[i, k], by_ss.at[i, k], by_rs.at[i, k],
                    device(x, zl, c, yy, zh),
                )
            )
        by_sent.append(row)

    def transpose(p, carry):
        for k in range(8):
            tiles_t[p * 8 + k] = tiles[p * 8 + k].T
        return carry

    lax.fori_loop(0, 16, transpose, 0)

    bz_sent = []
    own = None
    for i, dz in enumerate((2, 1, 3, 0)):
        total = part_b[i, y].astype(F32)
        for k in range(3):
            by_sent[i][k].wait_recv()
            total = total + recv_by[i, k].astype(F32)
        if dz:
            sum_z[i] = total.astype(BF16)
            bz_sent.append(
                send(
                    sum_z.at[i], recv_bz.at[i], bz_ss.at[i], bz_rs.at[i],
                    device(x, zl, c, y, (zh + dz) % 4),
                )
            )
        else:
            own = total

    def build_t(p, carry):
        place = (p // 4) * 4 + (p % 2) * 2 + (p // 2) % 2
        for q in range(16):
            r = (q % 4) * 4 + q // 4
            slot = slot_s[p, r]
            tile = tiles_t[p * 8 + jnp.minimum(slot, 7)]
            dense_t[place, :, q * T : (q + 1) * T] = jnp.where(
                slot < 8, tile, jnp.zeros_like(tile)
            )
        return carry

    lax.fori_loop(0, 16, build_t, 0)

    for i in range(3):
        bz_sent[i].wait_recv()
        own = own + recv_bz[i].astype(F32)

    inverse = recip[...]
    mean = (own * inverse).astype(BF16)
    pre = base[...] + dot(mean, wn[...])
    tanh = jnp.tanh(GELU_C * (pre + 0.044715 * (pre * pre * pre)))
    slope = 0.5 * (1.0 + tanh) + 0.5 * pre * (1.0 - tanh * tanh) * (
        GELU_C * (1.0 + 3.0 * 0.044715 * (pre * pre))
    )
    gp = (og_v[...].astype(F32) * slope).astype(BF16)
    me = zh * 4 + y
    grads_all[me] = (dot(gp, wn[...], 1, 1) * inverse).astype(BF16)

    cz_sent = []
    cy_sent = []
    for k, d in enumerate(FAR):
        cz_sent.append(
            send(
                grads_all.at[me], grads_all.at[me], cz_ss.at[k], cz_rs.at[k],
                device(x, zl, c, y, (zh + d) % 4),
            )
        )
    for k, d in enumerate(FAR):
        cy_sent.append(
            send(
                grads_all.at[me], grads_all.at[me], cy_ss.at[3, k], cy_rs.at[3, k],
                device(x, zl, c, (y + d) % 4, zh),
            )
        )

    out_v[...] = (0.5 * pre * (1.0 + tanh)).astype(BF16)
    store_out = pltpu.make_async_copy(out_v, out_h, local_sem.at[7])
    store_out.start()

    self_part = dot(feats_all[a], gp, 0, 0)
    neigh_part = dot(mean, gp, 0, 0)
    bias_part = jnp.sum(gp.astype(F32), axis=0, keepdims=True)
    first = c == 0
    ar1_s[0:W] = jnp.where(first, neigh_part, self_part).astype(BF16)
    ar1_s[W : W + 16] = bias_block(bias_part)
    r1 = send(ar1_s, ar1_r, r1_ss, r1_rs, sib)
    keep = jnp.where(first, self_part, neigh_part)
    self_keep[...] = dot(gp, ws[...], 1, 1)
    r1.wait_recv()
    chunk = keep + ar1_r[0:W].astype(F32)
    ar2_s[:, 0:16] = chunk.reshape(16, 16, W).astype(BF16)
    other = ar1_r[W : W + 16].astype(F32)
    mine = ar1_s[W : W + 16].astype(F32)
    both = jnp.sum(mine + other, axis=0, keepdims=True)
    ar2_s[:, 16:32] = jnp.broadcast_to(bias_block(both)[None], (16, 16, W))
    spot = x * 4 + y
    r2 = []
    for j, (dx, dy) in enumerate(PLANE):
        xx, yy = (x + dx) % 4, (y + dy) % 4
        r2.append(
            send(
                ar2_s.at[xx * 4 + yy], ar2_r.at[spot], r2_ss.at[j], r2_rs.at[j],
                device(xx, zl, c, yy, zh),
            )
        )
    ar2_r[spot] = ar2_s[spot]

    for k in (1, 2, 0):
        d = FAR[k]
        cz_sent[k].wait_recv()
        piece = ((zh - d) % 4) * 4 + y
        for m, dy in enumerate(FAR):
            cy_sent.append(
                send(
                    grads_all.at[piece], grads_all.at[piece], cy_ss.at[k, m], cy_rs.at[k, m],
                    device(x, zl, c, (y + dy) % 4, zh),
                )
            )

    for copy in r2:
        copy.wait_recv()
    total = jnp.zeros((32, W), F32)
    for j in range(16):
        total = total + ar2_r[j].astype(F32)
    ar3_s[0:16] = total[0:16].astype(BF16)
    ar3_s[16:32] = bias_block(jnp.sum(total[16:32], axis=0, keepdims=True))
    r3 = []
    for j in range(7):
        zz = (z + j + 1) % 8
        r3.append(
            send(
                ar3_s, ar3_r.at[z], r3_ss.at[j], r3_rs.at[j], device(x, zz % 2, c, y, zz // 2)
            )
        )
    ar3_r[z] = ar3_s[...]

    for copy in cy_sent:
        copy.wait_recv()

    grads = grads_all[...].reshape(16 * T, W)
    ds_sent = []
    for i, dx in enumerate((2, 1, 3, 0)):
        xx = (x + dx) % 4
        part = dot(dense_t[pl.ds(xx * 4, 4)].reshape(4 * T, 16 * T), grads)
        part_d[i] = part.reshape(2, 2, T, W).astype(BF16)
        ds_sent.append(send(part_d.at[i, 1 - c], recv_ds.at[i], ds_ss.at[i], ds_rs.at[i], sib))

    d_sent = []
    back = None
    for i, dx in enumerate((2, 1, 3, 0)):
        ds_sent[i].wait_recv()
        total = part_d[i, c].astype(F32) + recv_ds[i].astype(F32)
        sum_d[i] = total.astype(BF16)
        for dz in (1, 0):
            if dx or dz:
                xx, zz = chip(dx, dz)
                j = CHIPS.index((dx, dz))
                d_sent.append(
                    send(
                        sum_d.at[i, zz], recv_d.at[j], d_ss.at[j], d_rs.at[j],
                        device(xx, zz, c, y, zh),
                    )
                )
    back = self_keep[...] + sum_d[3, zl].astype(F32)

    for copy in r3:
        copy.wait_recv()
    total = jnp.zeros((32, W), F32)
    for j in range(8):
        total = total + ar3_r[j].astype(F32)
    bg_v[...] = jnp.sum(total[16:32], axis=0, keepdims=True)
    ar4[spot] = total[0:16].astype(BF16)
    r4 = []
    for j, (dx, dy) in enumerate(PLANE):
        xx, yy = (x + dx) % 4, (y + dy) % 4
        r4.append(
            send(
                ar4.at[spot], ar4.at[spot], r4_ss.at[j], r4_rs.at[j], device(xx, zl, c, yy, zh)
            )
        )
    for copy in r4:
        copy.wait_recv()
    r5 = send(ar4, ar5_r, r5_ss, r5_rs, sib)

    for copy in d_sent:
        copy.wait_recv()
    for j in range(7):
        back = back + recv_d[j].astype(F32)
    gf_v[...] = back.astype(BF16)
    store_gf = pltpu.make_async_copy(gf_v, gf_h, local_sem.at[8])
    store_gf.start()

    r5.wait_recv()
    here = ar4[...].reshape(W, W).astype(F32)
    there = ar5_r[...].reshape(W, W).astype(F32)
    sg_v[...] = jnp.where(first, here, there)
    ng_v[...] = jnp.where(first, there, here)
    stores = [
        store_out,
        store_gf,
        pltpu.make_async_copy(sg_v, sg_h, local_sem.at[9]),
        pltpu.make_async_copy(ng_v, ng_h, local_sem.at[10]),
        pltpu.make_async_copy(bg_v, bg_h, local_sem.at[11]),
    ]
    for store in stores[2:]:
        store.start()
    for store in stores:
        store.wait()
    for copy in sent:
        copy.wait_send()


def local(
    features, degrees, tile_values, tile_index, tile_count, self_weight, neigh_weight, bias,
    out_grad,
):
    index = tile_index[0, 0]
    count = tile_count[0, 0]
    slots = jnp.arange(8, dtype=jnp.int32)
    live = slots[None, :] < count[:, None]
    match = (index[:, :, None] == jnp.arange(16, dtype=jnp.int32)) & live[:, :, None]
    slot = jnp.min(jnp.where(match, slots[None, :, None], 8), axis=1)

    vm = pltpu.VMEM
    dma = pltpu.SemaphoreType.DMA
    anywhere = pl.BlockSpec(memory_space=pl.ANY)
    scratch = [
        vm((128, T, T), BF16), vm((128, T, T), BF16),
        vm((16, T, 16 * T), BF16), vm((16, T, 16 * T), BF16),
        vm((16, T, W), BF16), vm((16, T, W), BF16),
        vm((1, T), jnp.int32), vm((W, W), BF16), vm((W, W), BF16), vm((1, W), F32),
        vm((T, W), BF16),
        vm((T, W), F32), vm((T, W), F32),
        vm((4, 4, T, W), BF16), vm((4, 3, T, W), BF16), vm((3, T, W), BF16),
        vm((3, T, W), BF16),
        vm((T, W), BF16), vm((T, W), BF16), vm((T, W), BF16), vm((T, W), BF16), vm((T, W), F32),
        vm((4, 2, 2, T, W), BF16), vm((4, 2, T, W), BF16), vm((4, 2, T, W), BF16),
        vm((7, T, W), BF16),
        vm((W + 16, W), BF16), vm((W + 16, W), BF16),
        vm((16, 32, W), BF16), vm((16, 32, W), BF16),
        vm((32, W), BF16), vm((8, 32, W), BF16),
        vm((16, 16, W), BF16), vm((16, 16, W), BF16),
        vm((W, W), F32), vm((W, W), F32), vm((1, W), F32),
        dma((12,)), dma((8,)), dma((8,)), dma((7,)), dma((7,)),
        dma((4, 3)), dma((4, 3)), dma((3,)), dma((3,)),
        dma((3,)), dma((3,)), dma((4, 3)), dma((4, 3)),
        dma((4,)), dma((4,)), dma((7,)), dma((7,)),
        dma(()), dma(()), dma((15,)), dma((15,)), dma((7,)), dma((7,)),
        dma((15,)), dma((15,)), dma(()), dma(()),
    ]
    output, grad_features, self_grad, neigh_grad, bias_grad = pl.pallas_call(
        kernel,
        out_shape=(
            jax.ShapeDtypeStruct((T, W), BF16),
            jax.ShapeDtypeStruct((T, W), BF16),
            jax.ShapeDtypeStruct((W, W), F32),
            jax.ShapeDtypeStruct((W, W), F32),
            jax.ShapeDtypeStruct((1, W), F32),
        ),
        in_specs=[pl.BlockSpec(memory_space=pltpu.SMEM)] + [anywhere] * 7,
        out_specs=[anywhere] * 5,
        scratch_shapes=scratch,
        compiler_params=pltpu.CompilerParams(
            collective_id=0, has_side_effects=True, vmem_limit_bytes=56 * 2**20
        ),
        name="sage",
    )(
        slot,
        features,
        degrees.reshape(1, T),
        tile_values.reshape(128, T, T),
        self_weight,
        neigh_weight,
        bias.reshape(1, W),
        out_grad,
    )
    return output, grad_features, self_grad, neigh_grad, bias_grad.reshape(W)


def solution(mesh):
    placed = (
        P(("row", "col"), None),
        P(("row", "col")),
        P("row", "col", None, None, None, None),
        P("row", "col", None, None),
        P("row", "col", None),
        P(),
        P(),
        P(),
        P(("row", "col"), None),
    )
    return jax.shard_map(
        local,
        mesh=mesh,
        in_specs=placed,
        out_specs=(P(("row", "col"), None), P(("row", "col"), None), P(), P(), P()),
        check_vma=False,
    )
```

```python
import functools

import jax
import jax.numpy as jnp
from jax import lax
from jax.experimental import pallas as pl
from jax.experimental.pallas import tpu as pltpu
from jax.sharding import PartitionSpec as P

MESH = pl.DeviceIdType.MESH
F32 = jnp.float32
BF16 = jnp.bfloat16
T = 128
W = 256
CHIPS = [(dx, dz) for dx in (2, 1, 3, 0) for dz in (1, 0) if dx or dz]
PLANE = [(dx, dy) for dx in range(4) for dy in range(4) if dx or dy]
FAR = (2, 1, 3)
GELU_C = 0.7978845608028654


def dot(lhs, rhs, lhs_dim=1, rhs_dim=0):
    return lax.dot_general(
        lhs, rhs, (((lhs_dim,), (rhs_dim,)), ((), ())), preferred_element_type=F32
    )


def device(x, zl, c, y, zh):
    return (x * 4 + zl * 2 + c, y * 4 + zh)


def piece_at(x, zl, c):
    return x * 4 + c * 2 + zl


def split_rows(total):
    high = total.astype(BF16).astype(F32)
    return high, total - high


def bias_block(total):
    high, low = split_rows(total)
    line = lax.broadcasted_iota(jnp.int32, (16, W), 0)
    return jnp.where(line == 0, high, jnp.where(line == 1, low, 0.0)).astype(BF16)


def kernel(
    feats_h, deg_h, tiles_h, index_h, count_h, ws_h, wn_h, bias_h, og_h,
    out_v, gf_v, ar4, ar5_r, bg_v,
    tiles, dense, index_v, count_v, slot_v, slot_s, feats_all, grads_all,
    deg_v, ws, wn, bias_v, og_v, base, recip, part_b, recv_by, sum_z, recv_bz, self_keep,
    part_d, recv_ds, sum_d, recv_d, ar1_s, ar1_r, ar2_s, ar2_r, ar3_s, ar3_r,
    local_sem, a_ss, a_rs, af_ss, af_rs, by_ss, by_rs, bz_ss, bz_rs,
    cz_ss, cz_rs, cy_ss, cy_rs, ds_ss, ds_rs, d_ss, d_rs,
    r1_ss, r1_rs, r2_ss, r2_rs, r3_ss, r3_rs, r4_ss, r4_rs, r5_ss, r5_rs,
):
    a = lax.axis_index("row")
    b = lax.axis_index("col")
    x, zl, c = a // 4, (a // 2) % 2, a % 2
    y, zh = b // 4, b % 4
    z = zh * 2 + zl
    sib = device(x, zl, 1 - c, y, zh)
    home = piece_at(x, zl, c)
    sent = []

    def send(src, dst, send_sem, recv_sem, where):
        copy = pltpu.make_async_remote_copy(
            src_ref=src, dst_ref=dst, send_sem=send_sem, recv_sem=recv_sem,
            device_id=where, device_id_type=MESH,
        )
        copy.start()
        sent.append(copy)
        return copy

    def chip(dx, dz):
        return (x + dx) % 4, (zl + dz) % 2

    loads = [
        pltpu.make_async_copy(
            feats_h.at[:, pl.ds(h * T, T)], feats_all.at[h, home], local_sem.at[h]
        )
        for h in range(2)
    ]
    small = [
        pltpu.make_async_copy(index_h, index_v, local_sem.at[2]),
        pltpu.make_async_copy(count_h, count_v, local_sem.at[3]),
    ]
    large = [
        pltpu.make_async_copy(ws_h, ws, local_sem.at[4]),
        pltpu.make_async_copy(wn_h, wn, local_sem.at[5]),
        pltpu.make_async_copy(bias_h, bias_v, local_sem.at[6]),
        pltpu.make_async_copy(og_h, og_v, local_sem.at[7]),
        pltpu.make_async_copy(deg_h, deg_v, local_sem.at[8]),
        pltpu.make_async_copy(tiles_h, tiles, local_sem.at[9]),
    ]
    for load in loads + small + large:
        load.start()

    partners = [sib]
    partners += [device(*chip(dx, dz), c, y, zh) for dx, dz in CHIPS]
    partners += [device((x + dx) % 4, zl, c, (y + dy) % 4, zh) for dx, dy in PLANE if dy]
    partners += [
        device(x, zz % 2, c, y, zz // 2)
        for zz in [(z + d) % 8 for d in range(1, 8)]
    ]
    barrier = pltpu.get_barrier_semaphore()
    for partner in partners:
        pl.semaphore_signal(barrier, inc=1, device_id=partner, device_id_type=MESH)

    for load in small:
        load.wait()
    place = lax.broadcasted_iota(jnp.int32, (16, 16), 0)
    slot = jnp.full((16, 16), 8, jnp.int32)
    for k in range(8):
        here = (index_v[k : k + 1] == place) & (count_v[...] > k)
        slot = jnp.where(here, k, slot)
    slot_v[:, 0:16] = slot
    to_scalar = pltpu.make_async_copy(slot_v, slot_s, local_sem.at[10])
    to_scalar.start()
    for load in loads:
        load.wait()
    pl.semaphore_wait(barrier, len(partners))

    a_sent = []
    for h in range(2):
        mine = feats_all.at[h, home]
        a_sent.append(
            [
                send(mine, mine, a_ss.at[h, j], a_rs.at[h, j], device(*chip(dx, dz), c, y, zh))
                for j, (dx, dz) in enumerate(CHIPS)
            ]
            + [send(mine, mine, a_ss.at[h, 7], a_rs.at[h, 7], sib)]
        )

    to_scalar.wait()
    for load in large:
        load.wait()

    def build(q, carry):
        r = (q % 4) * 4 + q // 4
        for p in range(16):
            at = piece_at(p // 4, (p // 2) % 2, p % 2)
            slot = slot_s[r, p]
            tile = tiles[p * 8 + jnp.minimum(slot, 7)]
            dense[q, :, at * T : (at + 1) * T] = jnp.where(
                slot < 8, tile, jnp.zeros_like(tile)
            )
        return carry

    lax.fori_loop(0, 16, build, 0)
    feats = jnp.concatenate([feats_all[0, home], feats_all[1, home]], axis=1)
    base[...] = dot(feats, ws[...]) + bias_v[...]
    inverse = jnp.broadcast_to(1.0 / deg_v[...].astype(F32), (T, T)).T
    recip[...] = inverse

    by_sent = []
    for h in range(2):
        forwards = []
        for j in (4, 1, 3, 5, 6, 0, 2):
            dx, dz = CHIPS[j]
            a_sent[h][j].wait_recv()
            piece = feats_all.at[h, piece_at(*chip(-dx, dz), c)]
            forwards.append(send(piece, piece, af_ss.at[h, j], af_rs.at[h, j], sib))
        a_sent[h][7].wait_recv()
        for copy in forwards:
            copy.wait_recv()
        gathered = feats_all[h].reshape(16 * T, T)
        for i, dz in enumerate((2, 1, 3, 0)):
            zz = (zh + dz) % 4
            part = dot(dense[pl.ds(zz * 4, 4)].reshape(4 * T, 16 * T), gathered)
            part_b[h, i] = part.reshape(4, T, T).astype(BF16)
            row = []
            for k, dy in enumerate(FAR):
                yy = (y + dy) % 4
                row.append(
                    send(
                        part_b.at[h, i, yy], recv_by.at[h, i, k],
                        by_ss.at[h, i, k], by_rs.at[h, i, k], device(x, zl, c, yy, zh),
                    )
                )
            by_sent.append(row)

    bz_sent = []
    owns = []
    for h in range(2):
        for i, dz in enumerate((2, 1, 3, 0)):
            total = part_b[h, i, y].astype(F32)
            for k in range(3):
                by_sent[h * 4 + i][k].wait_recv()
                total = total + recv_by[h, i, k].astype(F32)
            if dz:
                sum_z[h, i] = total.astype(BF16)
                bz_sent.append(
                    send(
                        sum_z.at[h, i], recv_bz.at[h, i], bz_ss.at[h, i], bz_rs.at[h, i],
                        device(x, zl, c, y, (zh + dz) % 4),
                    )
                )
            else:
                owns.append(total)
    means = []
    pre = base[...]
    for h in range(2):
        total = owns[h]
        for i in range(3):
            bz_sent[h * 3 + i].wait_recv()
            total = total + recv_bz[h, i].astype(F32)
        means.append((total * recip[...]).astype(BF16))
        pre = pre + dot(means[h], wn[h * T : (h + 1) * T])

    tanh = jnp.tanh(GELU_C * (pre + 0.044715 * (pre * pre * pre)))
    slope = 0.5 * (1.0 + tanh) + 0.5 * pre * (1.0 - tanh * tanh) * (
        GELU_C * (1.0 + 3.0 * 0.044715 * (pre * pre))
    )
    gp = (og_v[...].astype(F32) * slope).astype(BF16)

    me = zh * 4 + y
    cz_sent = []
    cy_sent = [[], []]
    for h in range(2):
        mine = grads_all.at[h, me]
        grads_all[h, me] = (dot(gp, wn[h * T : (h + 1) * T], 1, 1) * recip[...]).astype(BF16)
        cz_sent.append(
            [
                send(
                    mine, mine, cz_ss.at[h, k], cz_rs.at[h, k],
                    device(x, zl, c, y, (zh + d) % 4),
                )
                for k, d in enumerate(FAR)
            ]
        )
        for k, d in enumerate(FAR):
            cy_sent[h].append(
                send(
                    mine, mine, cy_ss.at[h, 3, k], cy_rs.at[h, 3, k],
                    device(x, zl, c, (y + d) % 4, zh),
                )
            )

    out_v[...] = (0.5 * pre * (1.0 + tanh)).astype(BF16)

    mean = jnp.concatenate(means, axis=1)
    feats = jnp.concatenate([feats_all[0, home], feats_all[1, home]], axis=1)
    self_part = dot(feats, gp, 0, 0)
    neigh_part = dot(mean, gp, 0, 0)
    bias_part = jnp.sum(gp.astype(F32), axis=0, keepdims=True)
    first = c == 0
    ar1_s[0:W] = jnp.where(first, neigh_part, self_part).astype(BF16)
    ar1_s[W : W + 16] = bias_block(bias_part)
    r1 = send(ar1_s, ar1_r, r1_ss, r1_rs, sib)
    keep = jnp.where(first, self_part, neigh_part)
    self_keep[...] = dot(gp, ws[...], 1, 1)
    r1.wait_recv()
    chunk = keep + ar1_r[0:W].astype(F32)
    ar2_s[:, 0:16] = chunk.reshape(16, 16, W).astype(BF16)
    other = ar1_r[W : W + 16].astype(F32)
    mine = ar1_s[W : W + 16].astype(F32)
    both = jnp.sum(mine + other, axis=0, keepdims=True)
    ar2_s[:, 16:32] = jnp.broadcast_to(bias_block(both)[None], (16, 16, W))
    spot = x * 4 + y
    r2 = []
    for j, (dx, dy) in enumerate(PLANE):
        xx, yy = (x + dx) % 4, (y + dy) % 4
        r2.append(
            send(
                ar2_s.at[xx * 4 + yy], ar2_r.at[spot], r2_ss.at[j], r2_rs.at[j],
                device(xx, zl, c, yy, zh),
            )
        )
    ar2_r[spot] = ar2_s[spot]

    for h in range(2):
        for k in (1, 2, 0):
            cz_sent[h][k].wait_recv()
            piece = grads_all.at[h, ((zh - FAR[k]) % 4) * 4 + y]
            for m, dy in enumerate(FAR):
                cy_sent[h].append(
                    send(
                        piece, piece, cy_ss.at[h, k, m], cy_rs.at[h, k, m],
                        device(x, zl, c, (y + dy) % 4, zh),
                    )
                )

    for copy in r2:
        copy.wait_recv()
    total = jnp.zeros((32, W), F32)
    for j in range(16):
        total = total + ar2_r[j].astype(F32)
    ar3_s[0:16] = total[0:16].astype(BF16)
    ar3_s[16:32] = bias_block(jnp.sum(total[16:32], axis=0, keepdims=True))
    r3 = []
    for j in range(7):
        zz = (z + j + 1) % 8
        r3.append(
            send(
                ar3_s, ar3_r.at[z], r3_ss.at[j], r3_rs.at[j], device(x, zz % 2, c, y, zz // 2)
            )
        )
    ar3_r[z] = ar3_s[...]

    ds_sent = []
    d_sent = [[], []]

    def terms(h, i):
        xx = (x + (2, 1, 3, 0)[i]) % 4
        columns = pl.ds(pl.multiple_of(xx * 4 * T, 4 * T), 4 * T)
        block = dense[:, :, columns].reshape(16 * T, 4 * T)
        part = dot(block, grads_all[h].reshape(16 * T, T), 0, 0)
        part_d[h, i] = part.reshape(2, 2, T, T).astype(BF16)
        ds_sent.append(
            send(part_d.at[h, i, 1 - c], recv_ds.at[h, i], ds_ss.at[h, i], ds_rs.at[h, i], sib)
        )

    def pass_on(h, i):
        dx = (2, 1, 3, 0)[i]
        ds_sent[h * 4 + i].wait_recv()
        total = part_d[h, i, c].astype(F32) + recv_ds[h, i].astype(F32)
        sum_d[h, i] = total.astype(BF16)
        for dz in (1, 0):
            if dx or dz:
                xx, zz = chip(dx, dz)
                j = CHIPS.index((dx, dz))
                d_sent[h].append(
                    send(
                        sum_d.at[h, i, zz], recv_d.at[h, j], d_ss.at[h, j], d_rs.at[h, j],
                        device(xx, zz, c, y, zh),
                    )
                )

    for copy in cy_sent[0]:
        copy.wait_recv()
    for i in range(4):
        terms(0, i)
        if i:
            pass_on(0, i - 1)
    pass_on(0, 3)

    for copy in r3:
        copy.wait_recv()
    total = jnp.zeros((32, W), F32)
    for j in range(8):
        total = total + ar3_r[j].astype(F32)
    bg_v[...] = jnp.sum(total[16:32], axis=0, keepdims=True)
    ar4[spot] = total[0:16].astype(BF16)
    r4 = []
    for j, (dx, dy) in enumerate(PLANE):
        xx, yy = (x + dx) % 4, (y + dy) % 4
        r4.append(
            send(
                ar4.at[spot], ar4.at[spot], r4_ss.at[j], r4_rs.at[j], device(xx, zl, c, yy, zh)
            )
        )

    for copy in cy_sent[1]:
        copy.wait_recv()
    for i in range(4):
        terms(1, i)
        if i:
            pass_on(1, i - 1)
    pass_on(1, 3)

    for copy in r4:
        copy.wait_recv()
    r5 = send(ar4, ar5_r, r5_ss, r5_rs, sib)

    for h in range(2):
        back = self_keep[:, h * T : (h + 1) * T] + sum_d[h, 3, zl].astype(F32)
        for copy in d_sent[h]:
            copy.wait_recv()
        for j in range(7):
            back = back + recv_d[h, j].astype(F32)
        gf_v[:, h * T : (h + 1) * T] = back.astype(BF16)
    r5.wait_recv()
    for copy in sent:
        copy.wait_send()


def finish(out_v, gf_v, ar4, ar5_r, bg_v, out_h, gf_h, sg_h, ng_h, bg_h, sg_v, ng_v, sem):
    stores = [
        pltpu.make_async_copy(out_v, out_h, sem.at[0]),
        pltpu.make_async_copy(gf_v, gf_h, sem.at[1]),
        pltpu.make_async_copy(bg_v, bg_h, sem.at[2]),
        pltpu.make_async_copy(sg_v, sg_h, sem.at[3]),
        pltpu.make_async_copy(ng_v, ng_h, sem.at[4]),
    ]
    for store in stores[:3]:
        store.start()
    first = lax.axis_index("row") % 2 == 0
    here = ar4[...].reshape(W, W).astype(F32)
    there = ar5_r[...].reshape(W, W).astype(F32)
    sg_v[...] = jnp.where(first, here, there)
    stores[3].start()
    ng_v[...] = jnp.where(first, there, here)
    stores[4].start()
    for store in stores:
        store.wait()


def local(
    features, degrees, tile_values, tile_index, tile_count, self_weight, neigh_weight, bias,
    out_grad,
):
    vm = pltpu.VMEM
    dma = pltpu.SemaphoreType.DMA
    anywhere = pl.BlockSpec(memory_space=pl.ANY)
    inside = pl.BlockSpec(memory_space=pltpu.VMEM)
    scratch = [
        vm((128, T, T), BF16), vm((16, T, 16 * T), BF16),
        vm((8, 16), jnp.int32), vm((1, 16), jnp.int32), vm((16, T), jnp.int32),
        pltpu.SMEM((16, T), jnp.int32),
        vm((2, 16, T, T), BF16), vm((2, 16, T, T), BF16),
        vm((1, T), jnp.int32), vm((W, W), BF16), vm((W, W), BF16), vm((1, W), F32),
        vm((T, W), BF16),
        vm((T, W), F32), vm((T, T), F32),
        vm((2, 4, 4, T, T), BF16), vm((2, 4, 3, T, T), BF16), vm((2, 3, T, T), BF16),
        vm((2, 3, T, T), BF16), vm((T, W), F32),
        vm((2, 4, 2, 2, T, T), BF16), vm((2, 4, 2, T, T), BF16), vm((2, 4, 2, T, T), BF16),
        vm((2, 7, T, T), BF16),
        vm((W + 16, W), BF16), vm((W + 16, W), BF16),
        vm((16, 32, W), BF16), vm((16, 32, W), BF16),
        vm((32, W), BF16), vm((8, 32, W), BF16),
        dma((11,)), dma((2, 8)), dma((2, 8)), dma((2, 7)), dma((2, 7)),
        dma((2, 4, 3)), dma((2, 4, 3)), dma((2, 3)), dma((2, 3)),
        dma((2, 3)), dma((2, 3)), dma((2, 4, 3)), dma((2, 4, 3)),
        dma((2, 4)), dma((2, 4)), dma((2, 7)), dma((2, 7)),
        dma(()), dma(()), dma((15,)), dma((15,)), dma((7,)), dma((7,)),
        dma((15,)), dma((15,)), dma(()), dma(()),
    ]
    raw = pl.pallas_call(
        kernel,
        out_shape=(
            jax.ShapeDtypeStruct((T, W), BF16),
            jax.ShapeDtypeStruct((T, W), BF16),
            jax.ShapeDtypeStruct((16, 16, W), BF16),
            jax.ShapeDtypeStruct((16, 16, W), BF16),
            jax.ShapeDtypeStruct((1, W), F32),
        ),
        in_specs=[anywhere] * 9,
        out_specs=[inside] * 5,
        scratch_shapes=scratch,
        compiler_params=pltpu.CompilerParams(
            collective_id=0, has_side_effects=True, vmem_limit_bytes=58 * 2**20
        ),
        name="sage",
    )(
        features,
        degrees.reshape(1, T),
        tile_values.reshape(128, T, T),
        tile_index.reshape(16, 8).T,
        tile_count.reshape(1, 16),
        self_weight,
        neigh_weight,
        bias.reshape(1, W),
        out_grad,
    )
    output, grad_features, self_grad, neigh_grad, bias_grad = pl.pallas_call(
        finish,
        out_shape=(
            jax.ShapeDtypeStruct((T, W), BF16),
            jax.ShapeDtypeStruct((T, W), BF16),
            jax.ShapeDtypeStruct((W, W), F32),
            jax.ShapeDtypeStruct((W, W), F32),
            jax.ShapeDtypeStruct((1, W), F32),
        ),
        in_specs=[inside] * 5,
        out_specs=[anywhere] * 5,
        scratch_shapes=[vm((W, W), F32), vm((W, W), F32), dma((5,))],
        compiler_params=pltpu.CompilerParams(vmem_limit_bytes=62 * 2**20),
        name="finish",
    )(*raw)
    return output, grad_features, self_grad, neigh_grad, bias_grad.reshape(W)


def solution(mesh):
    placed = (
        P(("row", "col"), None),
        P(("row", "col")),
        P("row", "col", None, None, None, None),
        P("row", "col", None, None),
        P("row", "col", None),
        P(),
        P(),
        P(),
        P(("row", "col"), None),
    )
    return jax.shard_map(
        local,
        mesh=mesh,
        in_specs=placed,
        out_specs=(P(("row", "col"), None), P(("row", "col"), None), P(), P(), P()),
        check_vma=False,
    )
```

```python
import functools

import jax
import jax.numpy as jnp
from jax import lax
from jax.experimental import pallas as pl
from jax.experimental.pallas import tpu as pltpu
from jax.sharding import PartitionSpec as P

MESH = pl.DeviceIdType.MESH
F32 = jnp.float32
BF16 = jnp.bfloat16
T = 128
W = 256
CHIPS = [(dx, dz) for dx in (2, 1, 3, 0) for dz in (1, 0) if dx or dz]
PLANE = [(dx, dy) for dx in range(4) for dy in range(4) if dx or dy]
FAR = (2, 1, 3)
FAR_FIRST = (2, 1, 3, 0)
GELU_C = 0.7978845608028654


def dot(lhs, rhs, lhs_dim=1, rhs_dim=0):
    return lax.dot_general(
        lhs, rhs, (((lhs_dim,), (rhs_dim,)), ((), ())), preferred_element_type=F32
    )


def device(x, zl, c, y, zh):
    return (x * 4 + zl * 2 + c, y * 4 + zh)


def piece_at(x, zl, c):
    return c * 8 + x * 2 + zl


def split_rows(total):
    high = total.astype(BF16).astype(F32)
    return high, total - high


def bias_block(total):
    high, low = split_rows(total)
    line = lax.broadcasted_iota(jnp.int32, (16, W), 0)
    return jnp.where(line == 0, high, jnp.where(line == 1, low, 0.0)).astype(BF16)


def kernel(
    feats_h, deg_h, tiles_h, index_h, count_h, ws_h, wn_h, bias_h, og_h,
    out_v, gf_v, ar4, ar5_r, bg_v,
    tiles, dense, index_v, count_v, slot_v, slot_s, feats_all, grads_all,
    deg_v, ws, wn, bias_v, og_v, base, recip, sums, part_b, recv_by, sum_z, recv_bz, self_keep,
    part_d, keep_d, recv_ds, sum_d, recv_d, ar1_s, ar1_r, ar2_s, ar2_r, ar3_s, ar3_r,
    local_sem, a_ss, a_rs, af_ss, af_rs, by_ss, by_rs, bz_ss, bz_rs,
    cz_ss, cz_rs, cy_ss, cy_rs, ds_ss, ds_rs, d_ss, d_rs,
    r1_ss, r1_rs, r2_ss, r2_rs, r3_ss, r3_rs, r4_ss, r4_rs, r5_ss, r5_rs,
):
    a = lax.axis_index("row")
    b = lax.axis_index("col")
    x, zl, c = a // 4, (a // 2) % 2, a % 2
    y, zh = b // 4, b % 4
    z = zh * 2 + zl
    sib = device(x, zl, 1 - c, y, zh)
    home = piece_at(x, zl, c)
    sent = []

    def send(src, dst, send_sem, recv_sem, where):
        copy = pltpu.make_async_remote_copy(
            src_ref=src, dst_ref=dst, send_sem=send_sem, recv_sem=recv_sem,
            device_id=where, device_id_type=MESH,
        )
        copy.start()
        sent.append(copy)
        return copy

    def chip(dx, dz):
        return (x + dx) % 4, (zl + dz) % 2

    partners = [sib]
    partners += [device(*chip(dx, dz), c, y, zh) for dx, dz in CHIPS]
    partners += [device((x + dx) % 4, zl, c, (y + dy) % 4, zh) for dx, dy in PLANE if dy]
    partners += [
        device(x, zz % 2, c, y, zz // 2)
        for zz in [(z + d) % 8 for d in range(1, 8)]
    ]
    barrier = pltpu.get_barrier_semaphore()
    for partner in partners:
        pl.semaphore_signal(barrier, inc=1, device_id=partner, device_id_type=MESH)

    halves = [feats_h.at[:, pl.ds(h * T, T)] for h in range(2)]
    small = [
        pltpu.make_async_copy(index_h, index_v, local_sem.at[2]),
        pltpu.make_async_copy(count_h, count_v, local_sem.at[3]),
    ]
    large = [
        pltpu.make_async_copy(tiles_h, tiles, local_sem.at[9]),
        pltpu.make_async_copy(ws_h, ws, local_sem.at[4]),
        pltpu.make_async_copy(wn_h, wn, local_sem.at[5]),
        pltpu.make_async_copy(bias_h, bias_v, local_sem.at[6]),
        pltpu.make_async_copy(og_h, og_v, local_sem.at[7]),
        pltpu.make_async_copy(deg_h, deg_v, local_sem.at[8]),
    ]
    large += [
        pltpu.make_async_copy(halves[h], feats_all.at[h, home], local_sem.at[h])
        for h in range(2)
    ]
    for load in small + large:
        load.start()
    pl.semaphore_wait(barrier, len(partners))

    a_sent = []
    for h in range(2):
        there = feats_all.at[h, home]
        a_sent.append(
            [
                send(
                    halves[h], there, a_ss.at[h, j], a_rs.at[h, j],
                    device(*chip(dx, dz), c, y, zh),
                )
                for j, (dx, dz) in enumerate(CHIPS)
            ]
            + [send(halves[h], there, a_ss.at[h, 7], a_rs.at[h, 7], sib)]
        )

    for load in small:
        load.wait()
    place = lax.broadcasted_iota(jnp.int32, (16, 16), 0)
    slot = jnp.full((16, 16), 8, jnp.int32)
    for k in range(8):
        here = (index_v[k : k + 1] == place) & (count_v[...] > k)
        slot = jnp.where(here, k, slot)
    slot_v[:, 0:16] = slot
    to_scalar = pltpu.make_async_copy(slot_v, slot_s, local_sem.at[10])
    to_scalar.start()
    to_scalar.wait()
    for load in large:
        load.wait()

    def build(q, carry):
        r = (q % 4) * 4 + q // 4
        for p in range(16):
            at = piece_at(p // 4, (p // 2) % 2, p % 2)
            slot = slot_s[r, p]
            tile = tiles[p * 8 + jnp.minimum(slot, 7)]
            dense[q, :, at * T : (at + 1) * T] = jnp.where(
                slot < 8, tile, jnp.zeros_like(tile)
            )
        return carry

    lax.fori_loop(0, 16, build, 0)
    feats = jnp.concatenate([feats_all[0, home], feats_all[1, home]], axis=1)
    base[...] = dot(feats, ws[...]) + bias_v[...]
    inverse = jnp.broadcast_to(1.0 / deg_v[...].astype(F32), (T, T)).T
    recip[...] = inverse

    by_sent = []

    def shares(h, core, i):
        zz = (zh + FAR_FIRST[i]) % 4
        columns = pl.ds(pl.multiple_of(core * 8 * T, 8 * T), 8 * T)
        block = dense[pl.ds(zz * 4, 4), :, columns].reshape(4 * T, 8 * T)
        return dot(block, feats_all[h, pl.ds(core * 8, 8)].reshape(8 * T, T))

    for h in range(2):
        forwards = []
        for j in (4, 1, 3, 5, 6, 0, 2):
            dx, dz = CHIPS[j]
            a_sent[h][j].wait_recv()
            piece = feats_all.at[h, piece_at(*chip(-dx, dz), c)]
            forwards.append(send(piece, piece, af_ss.at[h, j], af_rs.at[h, j], sib))
        for i in range(4):
            sums[i] = shares(h, c, i)
        a_sent[h][7].wait_recv()
        for copy in forwards:
            copy.wait_recv()
        for i, dz in enumerate(FAR_FIRST):
            zz = (zh + dz) % 4
            part = sums[i] + shares(h, 1 - c, i)
            part_b[h, i] = part.reshape(4, T, T).astype(BF16)
            row = []
            for k, dy in enumerate(FAR):
                yy = (y + dy) % 4
                row.append(
                    send(
                        part_b.at[h, i, yy], recv_by.at[h, i, k],
                        by_ss.at[h, i, k], by_rs.at[h, i, k], device(x, zl, c, yy, zh),
                    )
                )
            by_sent.append(row)

    bz_sent = []
    owns = []
    for h in range(2):
        for i, dz in enumerate(FAR_FIRST):
            total = part_b[h, i, y].astype(F32)
            for k in range(3):
                by_sent[h * 4 + i][k].wait_recv()
                total = total + recv_by[h, i, k].astype(F32)
            if dz:
                sum_z[h, i] = total.astype(BF16)
                bz_sent.append(
                    send(
                        sum_z.at[h, i], recv_bz.at[h, i], bz_ss.at[h, i], bz_rs.at[h, i],
                        device(x, zl, c, y, (zh + dz) % 4),
                    )
                )
            else:
                owns.append(total)
    means = []
    pre = base[...]
    for h in range(2):
        total = owns[h]
        for i in range(3):
            bz_sent[h * 3 + i].wait_recv()
            total = total + recv_bz[h, i].astype(F32)
        means.append((total * recip[...]).astype(BF16))
        pre = pre + dot(means[h], wn[h * T : (h + 1) * T])

    tanh = jnp.tanh(GELU_C * (pre + 0.044715 * (pre * pre * pre)))
    slope = 0.5 * (1.0 + tanh) + 0.5 * pre * (1.0 - tanh * tanh) * (
        GELU_C * (1.0 + 3.0 * 0.044715 * (pre * pre))
    )
    gp = (og_v[...].astype(F32) * slope).astype(BF16)

    me = zh * 4 + y
    cz_sent = []
    cy_sent = [[], []]
    for h in range(2):
        mine = grads_all.at[h, me]
        grads_all[h, me] = (dot(gp, wn[h * T : (h + 1) * T], 1, 1) * recip[...]).astype(BF16)
        cz_sent.append(
            [
                send(
                    mine, mine, cz_ss.at[h, k], cz_rs.at[h, k],
                    device(x, zl, c, y, (zh + d) % 4),
                )
                for k, d in enumerate(FAR)
            ]
        )
        for k, d in enumerate(FAR):
            cy_sent[h].append(
                send(
                    mine, mine, cy_ss.at[h, 3, k], cy_rs.at[h, 3, k],
                    device(x, zl, c, (y + d) % 4, zh),
                )
            )

    out_v[...] = (0.5 * pre * (1.0 + tanh)).astype(BF16)

    mean = jnp.concatenate(means, axis=1)
    feats = jnp.concatenate([feats_all[0, home], feats_all[1, home]], axis=1)
    self_part = dot(feats, gp, 0, 0)
    neigh_part = dot(mean, gp, 0, 0)
    bias_part = jnp.sum(gp.astype(F32), axis=0, keepdims=True)
    first = c == 0
    ar1_s[0:W] = jnp.where(first, neigh_part, self_part).astype(BF16)
    ar1_s[W : W + 16] = bias_block(bias_part)
    r1 = send(ar1_s, ar1_r, r1_ss, r1_rs, sib)
    keep = jnp.where(first, self_part, neigh_part)
    self_keep[...] = dot(gp, ws[...], 1, 1)
    r1.wait_recv()
    chunk = keep + ar1_r[0:W].astype(F32)
    ar2_s[:, 0:16] = chunk.reshape(16, 16, W).astype(BF16)
    other = ar1_r[W : W + 16].astype(F32)
    mine = ar1_s[W : W + 16].astype(F32)
    both = jnp.sum(mine + other, axis=0, keepdims=True)
    ar2_s[:, 16:32] = jnp.broadcast_to(bias_block(both)[None], (16, 16, W))
    spot = x * 4 + y
    r2 = []
    for j, (dx, dy) in enumerate(PLANE):
        xx, yy = (x + dx) % 4, (y + dy) % 4
        r2.append(
            send(
                ar2_s.at[xx * 4 + yy], ar2_r.at[spot], r2_ss.at[j], r2_rs.at[j],
                device(xx, zl, c, yy, zh),
            )
        )
    ar2_r[spot] = ar2_s[spot]

    for h in range(2):
        for k in (1, 2, 0):
            cz_sent[h][k].wait_recv()
            piece = grads_all.at[h, ((zh - FAR[k]) % 4) * 4 + y]
            for m, dy in enumerate(FAR):
                cy_sent[h].append(
                    send(
                        piece, piece, cy_ss.at[h, k, m], cy_rs.at[h, k, m],
                        device(x, zl, c, (y + dy) % 4, zh),
                    )
                )

    for copy in r2:
        copy.wait_recv()
    total = jnp.zeros((32, W), F32)
    for j in range(16):
        total = total + ar2_r[j].astype(F32)
    ar3_s[0:16] = total[0:16].astype(BF16)
    ar3_s[16:32] = bias_block(jnp.sum(total[16:32], axis=0, keepdims=True))
    r3 = []
    for j in range(7):
        zz = (z + j + 1) % 8
        r3.append(
            send(
                ar3_s, ar3_r.at[z], r3_ss.at[j], r3_rs.at[j], device(x, zz % 2, c, y, zz // 2)
            )
        )
    ar3_r[z] = ar3_s[...]

    ds_sent = []
    d_sent = [[], []]

    def half_terms(h, core, i):
        at = core * 8 + (x + FAR_FIRST[i]) % 4 * 2
        columns = pl.ds(pl.multiple_of(at * T, 2 * T), 2 * T)
        block = dense[:, :, columns].reshape(16 * T, 2 * T)
        return dot(block, grads_all[h].reshape(16 * T, T), 0, 0).reshape(2, T, T)

    def terms(h, i):
        part_d[h, i] = half_terms(h, 1 - c, i).astype(BF16)
        ds_sent.append(
            send(part_d.at[h, i], recv_ds.at[h, i], ds_ss.at[h, i], ds_rs.at[h, i], sib)
        )
        keep_d[h, i] = half_terms(h, c, i)

    def pass_on(h, i):
        dx = FAR_FIRST[i]
        ds_sent[h * 4 + i].wait_recv()
        total = keep_d[h, i] + recv_ds[h, i].astype(F32)
        sum_d[h, i] = total.astype(BF16)
        for dz in (1, 0):
            if dx or dz:
                xx, zz = chip(dx, dz)
                j = CHIPS.index((dx, dz))
                d_sent[h].append(
                    send(
                        sum_d.at[h, i, zz], recv_d.at[h, j], d_ss.at[h, j], d_rs.at[h, j],
                        device(xx, zz, c, y, zh),
                    )
                )

    for copy in cy_sent[0]:
        copy.wait_recv()
    for i in range(4):
        terms(0, i)
        if i:
            pass_on(0, i - 1)
    pass_on(0, 3)

    for copy in r3:
        copy.wait_recv()
    total = jnp.zeros((32, W), F32)
    for j in range(8):
        total = total + ar3_r[j].astype(F32)
    bg_v[...] = jnp.sum(total[16:32], axis=0, keepdims=True)
    ar4[spot] = total[0:16].astype(BF16)
    r4 = []
    for j, (dx, dy) in enumerate(PLANE):
        xx, yy = (x + dx) % 4, (y + dy) % 4
        r4.append(
            send(
                ar4.at[spot], ar4.at[spot], r4_ss.at[j], r4_rs.at[j], device(xx, zl, c, yy, zh)
            )
        )

    for copy in cy_sent[1]:
        copy.wait_recv()
    for i in range(4):
        terms(1, i)
        if i:
            pass_on(1, i - 1)
    pass_on(1, 3)

    for copy in r4:
        copy.wait_recv()
    r5 = send(ar4, ar5_r, r5_ss, r5_rs, sib)

    for h in range(2):
        back = self_keep[:, h * T : (h + 1) * T] + sum_d[h, 3, zl].astype(F32)
        for copy in d_sent[h]:
            copy.wait_recv()
        for j in range(7):
            back = back + recv_d[h, j].astype(F32)
        gf_v[:, h * T : (h + 1) * T] = back.astype(BF16)
    r5.wait_recv()
    for copy in sent:
        copy.wait_send()


def finish(out_v, gf_v, ar4, ar5_r, bg_v, out_h, gf_h, sg_h, ng_h, bg_h, sg_v, ng_v, sem):
    stores = [
        pltpu.make_async_copy(out_v, out_h, sem.at[0]),
        pltpu.make_async_copy(gf_v, gf_h, sem.at[1]),
        pltpu.make_async_copy(bg_v, bg_h, sem.at[2]),
        pltpu.make_async_copy(sg_v, sg_h, sem.at[3]),
        pltpu.make_async_copy(ng_v, ng_h, sem.at[4]),
    ]
    for store in stores[:3]:
        store.start()
    first = lax.axis_index("row") % 2 == 0
    here = ar4[...].reshape(W, W).astype(F32)
    there = ar5_r[...].reshape(W, W).astype(F32)
    sg_v[...] = jnp.where(first, here, there)
    stores[3].start()
    ng_v[...] = jnp.where(first, there, here)
    stores[4].start()
    for store in stores:
        store.wait()


def local(
    features, degrees, tile_values, tile_index, tile_count, self_weight, neigh_weight, bias,
    out_grad,
):
    vm = pltpu.VMEM
    dma = pltpu.SemaphoreType.DMA
    anywhere = pl.BlockSpec(memory_space=pl.ANY)
    inside = pl.BlockSpec(memory_space=pltpu.VMEM)
    scratch = [
        vm((128, T, T), BF16), vm((16, T, 16 * T), BF16),
        vm((8, 16), jnp.int32), vm((1, 16), jnp.int32), vm((16, T), jnp.int32),
        pltpu.SMEM((16, T), jnp.int32),
        vm((2, 16, T, T), BF16), vm((2, 16, T, T), BF16),
        vm((1, T), jnp.int32), vm((W, W), BF16), vm((W, W), BF16), vm((1, W), F32),
        vm((T, W), BF16),
        vm((T, W), F32), vm((T, T), F32),
        vm((4, 4 * T, T), F32),
        vm((2, 4, 4, T, T), BF16), vm((2, 4, 3, T, T), BF16), vm((2, 3, T, T), BF16),
        vm((2, 3, T, T), BF16), vm((T, W), F32),
        vm((2, 4, 2, T, T), BF16), vm((2, 4, 2, T, T), F32), vm((2, 4, 2, T, T), BF16), vm((2, 4, 2, T, T), BF16),
        vm((2, 7, T, T), BF16),
        vm((W + 16, W), BF16), vm((W + 16, W), BF16),
        vm((16, 32, W), BF16), vm((16, 32, W), BF16),
        vm((32, W), BF16), vm((8, 32, W), BF16),
        dma((11,)), dma((2, 8)), dma((2, 8)), dma((2, 7)), dma((2, 7)),
        dma((2, 4, 3)), dma((2, 4, 3)), dma((2, 3)), dma((2, 3)),
        dma((2, 3)), dma((2, 3)), dma((2, 4, 3)), dma((2, 4, 3)),
        dma((2, 4)), dma((2, 4)), dma((2, 7)), dma((2, 7)),
        dma(()), dma(()), dma((15,)), dma((15,)), dma((7,)), dma((7,)),
        dma((15,)), dma((15,)), dma(()), dma(()),
    ]
    raw = pl.pallas_call(
        kernel,
        out_shape=(
            jax.ShapeDtypeStruct((T, W), BF16),
            jax.ShapeDtypeStruct((T, W), BF16),
            jax.ShapeDtypeStruct((16, 16, W), BF16),
            jax.ShapeDtypeStruct((16, 16, W), BF16),
            jax.ShapeDtypeStruct((1, W), F32),
        ),
        in_specs=[anywhere] * 9,
        out_specs=[inside] * 5,
        scratch_shapes=scratch,
        compiler_params=pltpu.CompilerParams(
            collective_id=0, has_side_effects=True, vmem_limit_bytes=58 * 2**20
        ),
        name="sage",
    )(
        features,
        degrees.reshape(1, T),
        tile_values.reshape(128, T, T),
        tile_index.reshape(16, 8).T,
        tile_count.reshape(1, 16),
        self_weight,
        neigh_weight,
        bias.reshape(1, W),
        out_grad,
    )
    output, grad_features, self_grad, neigh_grad, bias_grad = pl.pallas_call(
        finish,
        out_shape=(
            jax.ShapeDtypeStruct((T, W), BF16),
            jax.ShapeDtypeStruct((T, W), BF16),
            jax.ShapeDtypeStruct((W, W), F32),
            jax.ShapeDtypeStruct((W, W), F32),
            jax.ShapeDtypeStruct((1, W), F32),
        ),
        in_specs=[inside] * 5,
        out_specs=[anywhere] * 5,
        scratch_shapes=[vm((W, W), F32), vm((W, W), F32), dma((5,))],
        compiler_params=pltpu.CompilerParams(vmem_limit_bytes=62 * 2**20),
        name="finish",
    )(*raw)
    return output, grad_features, self_grad, neigh_grad, bias_grad.reshape(W)


def solution(mesh):
    placed = (
        P(("row", "col"), None),
        P(("row", "col")),
        P("row", "col", None, None, None, None),
        P("row", "col", None, None),
        P("row", "col", None),
        P(),
        P(),
        P(),
        P(("row", "col"), None),
    )
    return jax.shard_map(
        local,
        mesh=mesh,
        in_specs=placed,
        out_specs=(P(("row", "col"), None), P(("row", "col"), None), P(), P(), P()),
        check_vma=False,
    )
```

```python
import functools

import jax
import jax.numpy as jnp
from jax import lax
from jax.experimental import pallas as pl
from jax.experimental.pallas import tpu as pltpu
from jax.sharding import PartitionSpec as P

MESH = pl.DeviceIdType.MESH
F32 = jnp.float32
BF16 = jnp.bfloat16
T = 128
W = 256
CHIPS = [(dx, dz) for dx in (2, 1, 3, 0) for dz in (1, 0) if dx or dz]
PLANE = [(dx, dy) for dx in range(4) for dy in range(4) if dx or dy]
FAR = (2, 1, 3)
FAR_FIRST = (2, 1, 3, 0)
GELU_C = 0.7978845608028654


def dot(lhs, rhs, lhs_dim=1, rhs_dim=0):
    return lax.dot_general(
        lhs, rhs, (((lhs_dim,), (rhs_dim,)), ((), ())), preferred_element_type=F32
    )


def device(x, zl, c, y, zh):
    return (x * 4 + zl * 2 + c, y * 4 + zh)


def piece_at(x, zl, c):
    return c * 8 + x * 2 + zl


def split_rows(total):
    high = total.astype(BF16).astype(F32)
    return high, total - high


def bias_block(total):
    high, low = split_rows(total)
    line = lax.broadcasted_iota(jnp.int32, (16, W), 0)
    return jnp.where(line == 0, high, jnp.where(line == 1, low, 0.0)).astype(BF16)


def kernel(
    feats_h, deg_h, tiles_h, index_h, count_h, ws_h, wn_h, bias_h, og_h,
    out_h, gf_h, sg_h, ng_h, bg_h,
    out_v, gf_v, ar4, ar5_r, sg_v, ng_v, bg_v, tiles, dense, index_v, count_v, slot_v, slot_s, feats_all, grads_all,
    deg_v, ws, wn, bias_v, og_v, base, recip, sums, part_b, recv_by, sum_z, recv_bz, self_keep,
    part_d, keep_d, recv_ds, sum_d, recv_d, ar1_s, ar1_r, ar2_s, ar2_r, ar3_s, ar3_r,
    local_sem, a_ss, a_rs, af_ss, af_rs, by_ss, by_rs, bz_ss, bz_rs,
    cz_ss, cz_rs, cy_ss, cy_rs, ds_ss, ds_rs, d_ss, d_rs,
    r1_ss, r1_rs, r2_ss, r2_rs, r3_ss, r3_rs, r4_ss, r4_rs, r5_ss, r5_rs,
):
    a = lax.axis_index("row")
    b = lax.axis_index("col")
    x, zl, c = a // 4, (a // 2) % 2, a % 2
    y, zh = b // 4, b % 4
    z = zh * 2 + zl
    sib = device(x, zl, 1 - c, y, zh)
    home = piece_at(x, zl, c)
    sent = []

    def send(src, dst, send_sem, recv_sem, where):
        copy = pltpu.make_async_remote_copy(
            src_ref=src, dst_ref=dst, send_sem=send_sem, recv_sem=recv_sem,
            device_id=where, device_id_type=MESH,
        )
        copy.start()
        sent.append(copy)
        return copy

    def chip(dx, dz):
        return (x + dx) % 4, (zl + dz) % 2

    partners = [sib]
    partners += [device(*chip(dx, dz), c, y, zh) for dx, dz in CHIPS]
    partners += [device((x + dx) % 4, zl, c, (y + dy) % 4, zh) for dx, dy in PLANE if dy]
    partners += [
        device(x, zz % 2, c, y, zz // 2)
        for zz in [(z + d) % 8 for d in range(1, 8)]
    ]
    barrier = pltpu.get_barrier_semaphore()
    for partner in partners:
        pl.semaphore_signal(barrier, inc=1, device_id=partner, device_id_type=MESH)

    halves = [feats_h.at[:, pl.ds(h * T, T)] for h in range(2)]
    small = [
        pltpu.make_async_copy(index_h, index_v, local_sem.at[2]),
        pltpu.make_async_copy(count_h, count_v, local_sem.at[3]),
    ]
    large = [
        pltpu.make_async_copy(tiles_h, tiles, local_sem.at[9]),
        pltpu.make_async_copy(ws_h, ws, local_sem.at[4]),
        pltpu.make_async_copy(wn_h, wn, local_sem.at[5]),
        pltpu.make_async_copy(bias_h, bias_v, local_sem.at[6]),
        pltpu.make_async_copy(og_h, og_v, local_sem.at[7]),
        pltpu.make_async_copy(deg_h, deg_v, local_sem.at[8]),
    ]
    large += [
        pltpu.make_async_copy(halves[h], feats_all.at[h, home], local_sem.at[h])
        for h in range(2)
    ]
    for load in small + large:
        load.start()
    pl.semaphore_wait(barrier, len(partners))

    a_sent = []

    def send_half(h):
        there = feats_all.at[h, home]
        a_sent.append(
            [
                send(
                    halves[h], there, a_ss.at[h, j], a_rs.at[h, j],
                    device(*chip(dx, dz), c, y, zh),
                )
                for j, (dx, dz) in enumerate(CHIPS)
            ]
            + [send(halves[h], there, a_ss.at[h, 7], a_rs.at[h, 7], sib)]
        )

    send_half(0)

    for load in small:
        load.wait()
    place = lax.broadcasted_iota(jnp.int32, (16, 16), 0)
    slot = jnp.full((16, 16), 8, jnp.int32)
    for k in range(8):
        here = (index_v[k : k + 1] == place) & (count_v[...] > k)
        slot = jnp.where(here, k, slot)
    slot_v[:, 0:16] = slot
    to_scalar = pltpu.make_async_copy(slot_v, slot_s, local_sem.at[10])
    to_scalar.start()
    to_scalar.wait()
    for load in large:
        load.wait()

    def build(q, carry):
        r = (q % 4) * 4 + q // 4
        for p in range(16):
            at = piece_at(p // 4, (p // 2) % 2, p % 2)
            slot = slot_s[r, p]
            tile = tiles[p * 8 + jnp.minimum(slot, 7)]
            dense[q, :, at * T : (at + 1) * T] = jnp.where(
                slot < 8, tile, jnp.zeros_like(tile)
            )
        return carry

    lax.fori_loop(0, 16, build, 0)
    send_half(1)
    feats = jnp.concatenate([feats_all[0, home], feats_all[1, home]], axis=1)
    base[...] = dot(feats, ws[...]) + bias_v[...]
    inverse = jnp.broadcast_to(1.0 / deg_v[...].astype(F32), (T, T)).T
    recip[...] = inverse

    by_sent = []

    def shares(h, core, i):
        zz = (zh + FAR_FIRST[i]) % 4
        columns = pl.ds(pl.multiple_of(core * 8 * T, 8 * T), 8 * T)
        block = dense[pl.ds(zz * 4, 4), :, columns].reshape(4 * T, 8 * T)
        return dot(block, feats_all[h, pl.ds(core * 8, 8)].reshape(8 * T, T))

    for h in range(2):
        forwards = []
        for j in (4, 1, 3, 5, 6, 0, 2):
            dx, dz = CHIPS[j]
            a_sent[h][j].wait_recv()
            piece = feats_all.at[h, piece_at(*chip(-dx, dz), c)]
            forwards.append(send(piece, piece, af_ss.at[h, j], af_rs.at[h, j], sib))
        for i in range(4):
            sums[i] = shares(h, c, i)
        a_sent[h][7].wait_recv()
        for copy in forwards:
            copy.wait_recv()
        for i, dz in enumerate(FAR_FIRST):
            zz = (zh + dz) % 4
            part = sums[i] + shares(h, 1 - c, i)
            part_b[h, i] = part.reshape(4, T, T).astype(BF16)
            row = []
            for k, dy in enumerate(FAR):
                yy = (y + dy) % 4
                row.append(
                    send(
                        part_b.at[h, i, yy], recv_by.at[h, i, k],
                        by_ss.at[h, i, k], by_rs.at[h, i, k], device(x, zl, c, yy, zh),
                    )
                )
            by_sent.append(row)

    bz_sent = []
    owns = []
    for h in range(2):
        for i, dz in enumerate(FAR_FIRST):
            total = part_b[h, i, y].astype(F32)
            for k in range(3):
                by_sent[h * 4 + i][k].wait_recv()
                total = total + recv_by[h, i, k].astype(F32)
            if dz:
                sum_z[h, i] = total.astype(BF16)
                bz_sent.append(
                    send(
                        sum_z.at[h, i], recv_bz.at[h, i], bz_ss.at[h, i], bz_rs.at[h, i],
                        device(x, zl, c, y, (zh + dz) % 4),
                    )
                )
            else:
                owns.append(total)
    means = []
    pre = base[...]
    for h in range(2):
        total = owns[h]
        for i in range(3):
            bz_sent[h * 3 + i].wait_recv()
            total = total + recv_bz[h, i].astype(F32)
        means.append((total * recip[...]).astype(BF16))
        pre = pre + dot(means[h], wn[h * T : (h + 1) * T])

    tanh = jnp.tanh(GELU_C * (pre + 0.044715 * (pre * pre * pre)))
    slope = 0.5 * (1.0 + tanh) + 0.5 * pre * (1.0 - tanh * tanh) * (
        GELU_C * (1.0 + 3.0 * 0.044715 * (pre * pre))
    )
    gp = (og_v[...].astype(F32) * slope).astype(BF16)

    me = zh * 4 + y
    cz_sent = []
    cy_sent = [[], []]
    for h in range(2):
        mine = grads_all.at[h, me]
        grads_all[h, me] = (dot(gp, wn[h * T : (h + 1) * T], 1, 1) * recip[...]).astype(BF16)
        cz_sent.append(
            [
                send(
                    mine, mine, cz_ss.at[h, k], cz_rs.at[h, k],
                    device(x, zl, c, y, (zh + d) % 4),
                )
                for k, d in enumerate(FAR)
            ]
        )
        for k, d in enumerate(FAR):
            cy_sent[h].append(
                send(
                    mine, mine, cy_ss.at[h, 3, k], cy_rs.at[h, 3, k],
                    device(x, zl, c, (y + d) % 4, zh),
                )
            )

    out_v[...] = (0.5 * pre * (1.0 + tanh)).astype(BF16)
    stores = [pltpu.make_async_copy(out_v, out_h, local_sem.at[11])]
    stores[0].start()

    mean = jnp.concatenate(means, axis=1)
    feats = jnp.concatenate([feats_all[0, home], feats_all[1, home]], axis=1)
    self_part = dot(feats, gp, 0, 0)
    neigh_part = dot(mean, gp, 0, 0)
    bias_part = jnp.sum(gp.astype(F32), axis=0, keepdims=True)
    first = c == 0
    ar1_s[0:W] = jnp.where(first, neigh_part, self_part).astype(BF16)
    ar1_s[W : W + 16] = bias_block(bias_part)
    r1 = send(ar1_s, ar1_r, r1_ss, r1_rs, sib)
    keep = jnp.where(first, self_part, neigh_part)
    self_keep[...] = dot(gp, ws[...], 1, 1)
    r1.wait_recv()
    chunk = keep + ar1_r[0:W].astype(F32)
    ar2_s[:, 0:16] = chunk.reshape(16, 16, W).astype(BF16)
    other = ar1_r[W : W + 16].astype(F32)
    mine = ar1_s[W : W + 16].astype(F32)
    both = jnp.sum(mine + other, axis=0, keepdims=True)
    ar2_s[:, 16:32] = jnp.broadcast_to(bias_block(both)[None], (16, 16, W))
    spot = x * 4 + y
    r2 = []
    for j, (dx, dy) in enumerate(PLANE):
        xx, yy = (x + dx) % 4, (y + dy) % 4
        r2.append(
            send(
                ar2_s.at[xx * 4 + yy], ar2_r.at[spot], r2_ss.at[j], r2_rs.at[j],
                device(xx, zl, c, yy, zh),
            )
        )
    ar2_r[spot] = ar2_s[spot]

    for h in range(2):
        for k in (1, 2, 0):
            cz_sent[h][k].wait_recv()
            piece = grads_all.at[h, ((zh - FAR[k]) % 4) * 4 + y]
            for m, dy in enumerate(FAR):
                cy_sent[h].append(
                    send(
                        piece, piece, cy_ss.at[h, k, m], cy_rs.at[h, k, m],
                        device(x, zl, c, (y + dy) % 4, zh),
                    )
                )

    for copy in r2:
        copy.wait_recv()
    total = jnp.zeros((32, W), F32)
    for j in range(16):
        total = total + ar2_r[j].astype(F32)
    ar3_s[0:16] = total[0:16].astype(BF16)
    ar3_s[16:32] = bias_block(jnp.sum(total[16:32], axis=0, keepdims=True))
    r3 = []
    for j in range(7):
        zz = (z + j + 1) % 8
        r3.append(
            send(
                ar3_s, ar3_r.at[z], r3_ss.at[j], r3_rs.at[j], device(x, zz % 2, c, y, zz // 2)
            )
        )
    ar3_r[z] = ar3_s[...]

    ds_sent = []
    d_sent = [[], []]

    def half_terms(h, core, i):
        at = core * 8 + (x + FAR_FIRST[i]) % 4 * 2
        columns = pl.ds(pl.multiple_of(at * T, 2 * T), 2 * T)
        block = dense[:, :, columns].reshape(16 * T, 2 * T)
        return dot(block, grads_all[h].reshape(16 * T, T), 0, 0).reshape(2, T, T)

    def terms(h, i):
        part_d[h, i] = half_terms(h, 1 - c, i).astype(BF16)
        ds_sent.append(
            send(part_d.at[h, i], recv_ds.at[h, i], ds_ss.at[h, i], ds_rs.at[h, i], sib)
        )
        keep_d[h, i] = half_terms(h, c, i)

    def pass_on(h, i):
        dx = FAR_FIRST[i]
        ds_sent[h * 4 + i].wait_recv()
        total = keep_d[h, i] + recv_ds[h, i].astype(F32)
        sum_d[h, i] = total.astype(BF16)
        for dz in (1, 0):
            if dx or dz:
                xx, zz = chip(dx, dz)
                j = CHIPS.index((dx, dz))
                d_sent[h].append(
                    send(
                        sum_d.at[h, i, zz], recv_d.at[h, j], d_ss.at[h, j], d_rs.at[h, j],
                        device(xx, zz, c, y, zh),
                    )
                )

    for copy in cy_sent[0]:
        copy.wait_recv()
    for i in range(4):
        terms(0, i)
        if i:
            pass_on(0, i - 1)
    pass_on(0, 3)

    for copy in r3:
        copy.wait_recv()
    total = jnp.zeros((32, W), F32)
    for j in range(8):
        total = total + ar3_r[j].astype(F32)
    bg_v[...] = jnp.sum(total[16:32], axis=0, keepdims=True)
    ar4[spot] = total[0:16].astype(BF16)
    r4 = []
    for j, (dx, dy) in enumerate(PLANE):
        xx, yy = (x + dx) % 4, (y + dy) % 4
        r4.append(
            send(
                ar4.at[spot], ar4.at[spot], r4_ss.at[j], r4_rs.at[j], device(xx, zl, c, yy, zh)
            )
        )

    for copy in cy_sent[1]:
        copy.wait_recv()
    for i in range(4):
        terms(1, i)
        if i:
            pass_on(1, i - 1)
    pass_on(1, 3)

    for copy in r4:
        copy.wait_recv()
    r5 = send(ar4, ar5_r, r5_ss, r5_rs, sib)

    def total_back(h):
        back = self_keep[:, h * T : (h + 1) * T] + sum_d[h, 3, zl].astype(F32)
        for copy in d_sent[h]:
            copy.wait_recv()
        for j in range(7):
            back = back + recv_d[h, j].astype(F32)
        gf_v[:, h * T : (h + 1) * T] = back.astype(BF16)

    total_back(0)
    r5.wait_recv()
    here = ar4[...].reshape(W, W).astype(F32)
    there = ar5_r[...].reshape(W, W).astype(F32)
    sg_v[...] = jnp.where(first, here, there)
    ng_v[...] = jnp.where(first, there, here)
    stores += [
        pltpu.make_async_copy(sg_v, sg_h, local_sem.at[12]),
        pltpu.make_async_copy(ng_v, ng_h, local_sem.at[13]),
        pltpu.make_async_copy(bg_v, bg_h, local_sem.at[14]),
    ]
    for store in stores[1:]:
        store.start()
    for copy in sent:
        copy.wait_send()
    total_back(1)
    stores.append(pltpu.make_async_copy(gf_v, gf_h, local_sem.at[15]))
    stores[-1].start()
    for store in stores:
        store.wait()


def finish(*refs):
    stores = [
        pltpu.make_async_copy(refs[i], refs[5 + i], refs[10].at[i]) for i in range(5)
    ]
    for store in stores:
        store.start()
    for store in stores:
        store.wait()


def local(
    features, degrees, tile_values, tile_index, tile_count, self_weight, neigh_weight, bias,
    out_grad,
):
    vm = pltpu.VMEM
    dma = pltpu.SemaphoreType.DMA
    anywhere = pl.BlockSpec(memory_space=pl.ANY)
    scratch = [
        vm((T, W), BF16), vm((T, W), BF16), vm((16, 16, W), BF16), vm((16, 16, W), BF16),
        vm((W, W), F32), vm((W, W), F32), vm((1, W), F32),
        vm((128, T, T), BF16), vm((16, T, 16 * T), BF16),
        vm((8, 16), jnp.int32), vm((1, 16), jnp.int32), vm((16, T), jnp.int32),
        pltpu.SMEM((16, T), jnp.int32),
        vm((2, 16, T, T), BF16), vm((2, 16, T, T), BF16),
        vm((1, T), jnp.int32), vm((W, W), BF16), vm((W, W), BF16), vm((1, W), F32),
        vm((T, W), BF16),
        vm((T, W), F32), vm((T, T), F32),
        vm((4, 4 * T, T), F32),
        vm((2, 4, 4, T, T), BF16), vm((2, 4, 3, T, T), BF16), vm((2, 3, T, T), BF16),
        vm((2, 3, T, T), BF16), vm((T, W), F32),
        vm((2, 4, 2, T, T), BF16), vm((2, 4, 2, T, T), F32), vm((2, 4, 2, T, T), BF16), vm((2, 4, 2, T, T), BF16),
        vm((2, 7, T, T), BF16),
        vm((W + 16, W), BF16), vm((W + 16, W), BF16),
        vm((16, 32, W), BF16), vm((16, 32, W), BF16),
        vm((32, W), BF16), vm((8, 32, W), BF16),
        dma((16,)), dma((2, 8)), dma((2, 8)), dma((2, 7)), dma((2, 7)),
        dma((2, 4, 3)), dma((2, 4, 3)), dma((2, 3)), dma((2, 3)),
        dma((2, 3)), dma((2, 3)), dma((2, 4, 3)), dma((2, 4, 3)),
        dma((2, 4)), dma((2, 4)), dma((2, 7)), dma((2, 7)),
        dma(()), dma(()), dma((15,)), dma((15,)), dma((7,)), dma((7,)),
        dma((15,)), dma((15,)), dma(()), dma(()),
    ]
    shapes = (
        jax.ShapeDtypeStruct((T, W), BF16),
        jax.ShapeDtypeStruct((T, W), BF16),
        jax.ShapeDtypeStruct((W, W), F32),
        jax.ShapeDtypeStruct((W, W), F32),
        jax.ShapeDtypeStruct((1, W), F32),
    )
    raw = pl.pallas_call(
        kernel,
        out_shape=shapes,
        in_specs=[anywhere] * 9,
        out_specs=[anywhere] * 5,
        scratch_shapes=scratch,
        compiler_params=pltpu.CompilerParams(
            collective_id=0, has_side_effects=True, vmem_limit_bytes=58 * 2**20
        ),
        name="sage",
    )(
        features,
        degrees.reshape(1, T),
        tile_values.reshape(128, T, T),
        tile_index.reshape(16, 8).T,
        tile_count.reshape(1, 16),
        self_weight,
        neigh_weight,
        bias.reshape(1, W),
        out_grad,
    )
    output, grad_features, self_grad, neigh_grad, bias_grad = pl.pallas_call(
        finish,
        out_shape=shapes,
        in_specs=[pl.BlockSpec(memory_space=pltpu.VMEM)] * 5,
        out_specs=[anywhere] * 5,
        scratch_shapes=[dma((5,))],
        compiler_params=pltpu.CompilerParams(vmem_limit_bytes=62 * 2**20),
        name="finish",
    )(*raw)
    return output, grad_features, self_grad, neigh_grad, bias_grad.reshape(W)


def solution(mesh):
    placed = (
        P(("row", "col"), None),
        P(("row", "col")),
        P("row", "col", None, None, None, None),
        P("row", "col", None, None),
        P("row", "col", None),
        P(),
        P(),
        P(),
        P(("row", "col"), None),
    )
    return jax.shard_map(
        local,
        mesh=mesh,
        in_specs=placed,
        out_specs=(P(("row", "col"), None), P(("row", "col"), None), P(), P(), P()),
        check_vma=False,
    )
```

```python
import functools

import jax
import jax.numpy as jnp
from jax import lax
from jax.experimental import pallas as pl
from jax.experimental.pallas import tpu as pltpu
from jax.sharding import PartitionSpec as P

MESH = pl.DeviceIdType.MESH
F32 = jnp.float32
BF16 = jnp.bfloat16
T = 128
W = 256
CHIPS = [(dx, dz) for dx in (2, 1, 3, 0) for dz in (1, 0) if dx or dz]
PLANE = [(dx, dy) for dx in range(4) for dy in range(4) if dx or dy]
FAR = (1, 3, 2)
FAR_FIRST = (2, 1, 3, 0)
GELU_C = 0.7978845608028654


def dot(lhs, rhs, lhs_dim=1, rhs_dim=0):
    return lax.dot_general(
        lhs, rhs, (((lhs_dim,), (rhs_dim,)), ((), ())), preferred_element_type=F32
    )


def device(x, zl, c, y, zh):
    return (x * 4 + zl * 2 + c, y * 4 + zh)


def piece_at(x, zl, c):
    return c * 8 + x * 2 + zl


def split_rows(total):
    high = total.astype(BF16).astype(F32)
    return high, total - high


def bias_block(total):
    high, low = split_rows(total)
    line = lax.broadcasted_iota(jnp.int32, (16, W), 0)
    return jnp.where(line == 0, high, jnp.where(line == 1, low, 0.0)).astype(BF16)


def kernel(
    feats_h, deg_h, tiles_h, index_h, count_h, ws_h, wn_h, bias_h, og_h,
    out_h, gf_h, sg_h, ng_h, bg_h,
    out_v, gf_v, ar4, ar5_r, sg_v, ng_v, bg_v, tiles, dense, index_v, count_v, slot_v, slot_s, feats_all, grads_all,
    deg_v, ws, wn, bias_v, og_v, base, recip, sums, part_b, recv_by, sum_z, recv_bz, self_keep,
    part_d, keep_d, recv_ds, sum_d, recv_d, ar1_s, ar1_r, ar2_s, ar2_r, ar3_s, ar3_r,
    local_sem, a_ss, a_rs, af_ss, af_rs, by_ss, by_rs, bz_ss, bz_rs,
    cz_ss, cz_rs, cy_ss, cy_rs, ds_ss, ds_rs, d_ss, d_rs,
    r1_ss, r1_rs, r2_ss, r2_rs, r3_ss, r3_rs, r4_ss, r4_rs, r5_ss, r5_rs,
):
    a = lax.axis_index("row")
    b = lax.axis_index("col")
    x, zl, c = a // 4, (a // 2) % 2, a % 2
    y, zh = b // 4, b % 4
    z = zh * 2 + zl
    sib = device(x, zl, 1 - c, y, zh)
    home = piece_at(x, zl, c)
    sent = []

    def send(src, dst, send_sem, recv_sem, where):
        copy = pltpu.make_async_remote_copy(
            src_ref=src, dst_ref=dst, send_sem=send_sem, recv_sem=recv_sem,
            device_id=where, device_id_type=MESH,
        )
        copy.start()
        sent.append(copy)
        return copy

    def chip(dx, dz):
        return (x + dx) % 4, (zl + dz) % 2

    partners = [sib]
    partners += [device(*chip(dx, dz), c, y, zh) for dx, dz in CHIPS]
    partners += [device((x + dx) % 4, zl, c, (y + dy) % 4, zh) for dx, dy in PLANE if dy]
    partners += [
        device(x, zz % 2, c, y, zz // 2)
        for zz in [(z + d) % 8 for d in range(1, 8)]
    ]
    barrier = pltpu.get_barrier_semaphore()
    for partner in reversed(partners):
        pl.semaphore_signal(barrier, inc=1, device_id=partner, device_id_type=MESH)

    halves = [feats_h.at[:, pl.ds(h * T, T)] for h in range(2)]
    small = [
        pltpu.make_async_copy(index_h, index_v, local_sem.at[2]),
        pltpu.make_async_copy(count_h, count_v, local_sem.at[3]),
    ]
    large = [
        pltpu.make_async_copy(tiles_h, tiles, local_sem.at[9]),
        pltpu.make_async_copy(ws_h, ws, local_sem.at[4]),
        pltpu.make_async_copy(wn_h, wn, local_sem.at[5]),
        pltpu.make_async_copy(bias_h, bias_v, local_sem.at[6]),
        pltpu.make_async_copy(og_h, og_v, local_sem.at[7]),
        pltpu.make_async_copy(deg_h, deg_v, local_sem.at[8]),
    ]
    large += [
        pltpu.make_async_copy(halves[h], feats_all.at[h, home], local_sem.at[h])
        for h in range(2)
    ]
    for load in small + large:
        load.start()
    pl.semaphore_wait(barrier, len(partners))

    a_sent = []

    def send_half(h):
        there = feats_all.at[h, home]
        a_sent.append(
            [
                send(
                    halves[h], there, a_ss.at[h, j], a_rs.at[h, j],
                    device(*chip(dx, dz), c, y, zh),
                )
                for j, (dx, dz) in enumerate(CHIPS)
            ]
            + [send(halves[h], there, a_ss.at[h, 7], a_rs.at[h, 7], sib)]
        )

    send_half(0)

    for load in small:
        load.wait()
    place = lax.broadcasted_iota(jnp.int32, (16, 16), 0)
    slot = jnp.full((16, 16), 8, jnp.int32)
    for k in range(8):
        here = (index_v[k : k + 1] == place) & (count_v[...] > k)
        slot = jnp.where(here, k, slot)
    slot_v[:, 0:16] = slot
    to_scalar = pltpu.make_async_copy(slot_v, slot_s, local_sem.at[10])
    to_scalar.start()
    to_scalar.wait()
    for load in large:
        load.wait()

    def build(q, carry):
        r = (q % 4) * 4 + q // 4
        for p in range(16):
            at = piece_at(p // 4, (p // 2) % 2, p % 2)
            slot = slot_s[r, p]
            tile = tiles[p * 8 + jnp.minimum(slot, 7)]
            dense[q, :, at * T : (at + 1) * T] = jnp.where(
                slot < 8, tile, jnp.zeros_like(tile)
            )
        return carry

    lax.fori_loop(0, 16, build, 0)
    send_half(1)
    feats = jnp.concatenate([feats_all[0, home], feats_all[1, home]], axis=1)
    base[...] = dot(feats, ws[...]) + bias_v[...]
    inverse = jnp.broadcast_to(1.0 / deg_v[...].astype(F32), (T, T)).T
    recip[...] = inverse

    by_sent = []

    def shares(h, core, i):
        zz = (zh + FAR_FIRST[i]) % 4
        columns = pl.ds(pl.multiple_of(core * 8 * T, 8 * T), 8 * T)
        block = dense[pl.ds(zz * 4, 4), :, columns].reshape(4 * T, 8 * T)
        return dot(block, feats_all[h, pl.ds(core * 8, 8)].reshape(8 * T, T))

    for h in range(2):
        forwards = []
        for j in (6, 3, 5, 1, 2, 4, 0):
            dx, dz = CHIPS[j]
            a_sent[h][j].wait_recv()
            piece = feats_all.at[h, piece_at(*chip(-dx, dz), c)]
            forwards.append(send(piece, piece, af_ss.at[h, j], af_rs.at[h, j], sib))
        for i in range(4):
            sums[i] = shares(h, c, i)
        a_sent[h][7].wait_recv()
        for copy in forwards:
            copy.wait_recv()
        for i, dz in enumerate(FAR_FIRST):
            zz = (zh + dz) % 4
            part = sums[i] + shares(h, 1 - c, i)
            part_b[h, i] = part.reshape(4, T, T).astype(BF16)
            row = []
            for k, dy in enumerate(FAR):
                yy = (y + dy) % 4
                row.append(
                    send(
                        part_b.at[h, i, yy], recv_by.at[h, i, k],
                        by_ss.at[h, i, k], by_rs.at[h, i, k], device(x, zl, c, yy, zh),
                    )
                )
            by_sent.append(row)

    bz_sent = []
    owns = []
    for h in range(2):
        for i, dz in enumerate(FAR_FIRST):
            total = part_b[h, i, y].astype(F32)
            for k in range(3):
                by_sent[h * 4 + i][k].wait_recv()
                total = total + recv_by[h, i, k].astype(F32)
            if dz:
                sum_z[h, i] = total.astype(BF16)
                bz_sent.append(
                    send(
                        sum_z.at[h, i], recv_bz.at[h, i], bz_ss.at[h, i], bz_rs.at[h, i],
                        device(x, zl, c, y, (zh + dz) % 4),
                    )
                )
            else:
                owns.append(total)
    means = []
    pre = base[...]
    for h in range(2):
        total = owns[h]
        for i in range(3):
            bz_sent[h * 3 + i].wait_recv()
            total = total + recv_bz[h, i].astype(F32)
        means.append((total * recip[...]).astype(BF16))
        pre = pre + dot(means[h], wn[h * T : (h + 1) * T])

    tanh = jnp.tanh(GELU_C * (pre + 0.044715 * (pre * pre * pre)))
    slope = 0.5 * (1.0 + tanh) + 0.5 * pre * (1.0 - tanh * tanh) * (
        GELU_C * (1.0 + 3.0 * 0.044715 * (pre * pre))
    )
    gp = (og_v[...].astype(F32) * slope).astype(BF16)

    me = zh * 4 + y
    cz_sent = []
    cy_sent = [[], []]
    for h in range(2):
        mine = grads_all.at[h, me]
        grads_all[h, me] = (dot(gp, wn[h * T : (h + 1) * T], 1, 1) * recip[...]).astype(BF16)
        cz_sent.append(
            [
                send(
                    mine, mine, cz_ss.at[h, k], cz_rs.at[h, k],
                    device(x, zl, c, y, (zh + d) % 4),
                )
                for k, d in enumerate(FAR)
            ]
        )
        for k, d in enumerate(FAR):
            cy_sent[h].append(
                send(
                    mine, mine, cy_ss.at[h, 3, k], cy_rs.at[h, 3, k],
                    device(x, zl, c, (y + d) % 4, zh),
                )
            )

    out_v[...] = (0.5 * pre * (1.0 + tanh)).astype(BF16)
    stores = [pltpu.make_async_copy(out_v, out_h, local_sem.at[11])]
    stores[0].start()

    mean = jnp.concatenate(means, axis=1)
    feats = jnp.concatenate([feats_all[0, home], feats_all[1, home]], axis=1)
    self_part = dot(feats, gp, 0, 0)
    neigh_part = dot(mean, gp, 0, 0)
    bias_part = jnp.sum(gp.astype(F32), axis=0, keepdims=True)
    first = c == 0
    ar1_s[0:W] = jnp.where(first, neigh_part, self_part).astype(BF16)
    ar1_s[W : W + 16] = bias_block(bias_part)
    r1 = send(ar1_s, ar1_r, r1_ss, r1_rs, sib)
    keep = jnp.where(first, self_part, neigh_part)
    self_keep[...] = dot(gp, ws[...], 1, 1)
    r1.wait_recv()
    chunk = keep + ar1_r[0:W].astype(F32)
    ar2_s[:, 0:16] = chunk.reshape(16, 16, W).astype(BF16)
    other = ar1_r[W : W + 16].astype(F32)
    mine = ar1_s[W : W + 16].astype(F32)
    both = jnp.sum(mine + other, axis=0, keepdims=True)
    ar2_s[:, 16:32] = jnp.broadcast_to(bias_block(both)[None], (16, 16, W))
    spot = x * 4 + y
    r2 = []
    for j, (dx, dy) in enumerate(PLANE):
        xx, yy = (x + dx) % 4, (y + dy) % 4
        r2.append(
            send(
                ar2_s.at[xx * 4 + yy], ar2_r.at[spot], r2_ss.at[j], r2_rs.at[j],
                device(xx, zl, c, yy, zh),
            )
        )
    ar2_r[spot] = ar2_s[spot]

    for h in range(2):
        for k in range(3):
            cz_sent[h][k].wait_recv()
            piece = grads_all.at[h, ((zh - FAR[k]) % 4) * 4 + y]
            for m, dy in enumerate(FAR):
                cy_sent[h].append(
                    send(
                        piece, piece, cy_ss.at[h, k, m], cy_rs.at[h, k, m],
                        device(x, zl, c, (y + dy) % 4, zh),
                    )
                )

    for copy in r2:
        copy.wait_recv()
    total = jnp.zeros((32, W), F32)
    for j in range(16):
        total = total + ar2_r[j].astype(F32)
    ar3_s[0:16] = total[0:16].astype(BF16)
    ar3_s[16:32] = bias_block(jnp.sum(total[16:32], axis=0, keepdims=True))
    r3 = []
    for j in range(7):
        zz = (z + j + 1) % 8
        r3.append(
            send(
                ar3_s, ar3_r.at[z], r3_ss.at[j], r3_rs.at[j], device(x, zz % 2, c, y, zz // 2)
            )
        )
    ar3_r[z] = ar3_s[...]

    ds_sent = []
    d_sent = [[], []]

    def half_terms(h, core, i):
        at = core * 8 + (x + FAR_FIRST[i]) % 4 * 2
        columns = pl.ds(pl.multiple_of(at * T, 2 * T), 2 * T)
        block = dense[:, :, columns].reshape(16 * T, 2 * T)
        return dot(block, grads_all[h].reshape(16 * T, T), 0, 0).reshape(2, T, T)

    def terms(h, i):
        part_d[h, i] = half_terms(h, 1 - c, i).astype(BF16)
        ds_sent.append(
            send(part_d.at[h, i], recv_ds.at[h, i], ds_ss.at[h, i], ds_rs.at[h, i], sib)
        )
        keep_d[h, i] = half_terms(h, c, i)

    def pass_on(h, i):
        dx = FAR_FIRST[i]
        ds_sent[h * 4 + i].wait_recv()
        total = keep_d[h, i] + recv_ds[h, i].astype(F32)
        sum_d[h, i] = total.astype(BF16)
        for dz in (1, 0):
            if dx or dz:
                xx, zz = chip(dx, dz)
                j = CHIPS.index((dx, dz))
                d_sent[h].append(
                    send(
                        sum_d.at[h, i, zz], recv_d.at[h, j], d_ss.at[h, j], d_rs.at[h, j],
                        device(xx, zz, c, y, zh),
                    )
                )

    for copy in cy_sent[0]:
        copy.wait_recv()
    for i in range(4):
        terms(0, i)
        if i:
            pass_on(0, i - 1)
    pass_on(0, 3)

    for copy in r3:
        copy.wait_recv()
    total = jnp.zeros((32, W), F32)
    for j in range(8):
        total = total + ar3_r[j].astype(F32)
    bg_v[...] = jnp.sum(total[16:32], axis=0, keepdims=True)
    ar4[spot] = total[0:16].astype(BF16)
    r4 = []
    for j, (dx, dy) in enumerate(PLANE):
        xx, yy = (x + dx) % 4, (y + dy) % 4
        r4.append(
            send(
                ar4.at[spot], ar4.at[spot], r4_ss.at[j], r4_rs.at[j], device(xx, zl, c, yy, zh)
            )
        )

    for copy in cy_sent[1]:
        copy.wait_recv()
    for i in range(4):
        terms(1, i)
        if i:
            pass_on(1, i - 1)
    pass_on(1, 3)

    for copy in r4:
        copy.wait_recv()
    r5 = send(ar4, ar5_r, r5_ss, r5_rs, sib)

    def total_back(h):
        back = self_keep[:, h * T : (h + 1) * T] + sum_d[h, 3, zl].astype(F32)
        for copy in d_sent[h]:
            copy.wait_recv()
        for j in range(7):
            back = back + recv_d[h, j].astype(F32)
        gf_v[:, h * T : (h + 1) * T] = back.astype(BF16)

    total_back(0)
    r5.wait_recv()
    here = ar4[...].reshape(W, W).astype(F32)
    there = ar5_r[...].reshape(W, W).astype(F32)
    sg_v[...] = jnp.where(first, here, there)
    ng_v[...] = jnp.where(first, there, here)
    stores += [
        pltpu.make_async_copy(sg_v, sg_h, local_sem.at[12]),
        pltpu.make_async_copy(ng_v, ng_h, local_sem.at[13]),
        pltpu.make_async_copy(bg_v, bg_h, local_sem.at[14]),
    ]
    for store in stores[1:]:
        store.start()
    for copy in sent:
        copy.wait_send()
    total_back(1)
    stores.append(pltpu.make_async_copy(gf_v, gf_h, local_sem.at[15]))
    stores[-1].start()
    for store in stores:
        store.wait()


def finish(*refs):
    stores = [
        pltpu.make_async_copy(refs[i], refs[5 + i], refs[10].at[i]) for i in range(5)
    ]
    for store in stores:
        store.start()
    for store in stores:
        store.wait()


def local(
    features, degrees, tile_values, tile_index, tile_count, self_weight, neigh_weight, bias,
    out_grad,
):
    vm = pltpu.VMEM
    dma = pltpu.SemaphoreType.DMA
    anywhere = pl.BlockSpec(memory_space=pl.ANY)
    scratch = [
        vm((T, W), BF16), vm((T, W), BF16), vm((16, 16, W), BF16), vm((16, 16, W), BF16),
        vm((W, W), F32), vm((W, W), F32), vm((1, W), F32),
        vm((128, T, T), BF16), vm((16, T, 16 * T), BF16),
        vm((8, 16), jnp.int32), vm((1, 16), jnp.int32), vm((16, T), jnp.int32),
        pltpu.SMEM((16, T), jnp.int32),
        vm((2, 16, T, T), BF16), vm((2, 16, T, T), BF16),
        vm((1, T), jnp.int32), vm((W, W), BF16), vm((W, W), BF16), vm((1, W), F32),
        vm((T, W), BF16),
        vm((T, W), F32), vm((T, T), F32),
        vm((4, 4 * T, T), F32),
        vm((2, 4, 4, T, T), BF16), vm((2, 4, 3, T, T), BF16), vm((2, 3, T, T), BF16),
        vm((2, 3, T, T), BF16), vm((T, W), F32),
        vm((2, 4, 2, T, T), BF16), vm((2, 4, 2, T, T), F32), vm((2, 4, 2, T, T), BF16), vm((2, 4, 2, T, T), BF16),
        vm((2, 7, T, T), BF16),
        vm((W + 16, W), BF16), vm((W + 16, W), BF16),
        vm((16, 32, W), BF16), vm((16, 32, W), BF16),
        vm((32, W), BF16), vm((8, 32, W), BF16),
        dma((16,)), dma((2, 8)), dma((2, 8)), dma((2, 7)), dma((2, 7)),
        dma((2, 4, 3)), dma((2, 4, 3)), dma((2, 3)), dma((2, 3)),
        dma((2, 3)), dma((2, 3)), dma((2, 4, 3)), dma((2, 4, 3)),
        dma((2, 4)), dma((2, 4)), dma((2, 7)), dma((2, 7)),
        dma(()), dma(()), dma((15,)), dma((15,)), dma((7,)), dma((7,)),
        dma((15,)), dma((15,)), dma(()), dma(()),
    ]
    shapes = (
        jax.ShapeDtypeStruct((T, W), BF16),
        jax.ShapeDtypeStruct((T, W), BF16),
        jax.ShapeDtypeStruct((W, W), F32),
        jax.ShapeDtypeStruct((W, W), F32),
        jax.ShapeDtypeStruct((1, W), F32),
    )
    raw = pl.pallas_call(
        kernel,
        out_shape=shapes,
        in_specs=[anywhere] * 9,
        out_specs=[anywhere] * 5,
        scratch_shapes=scratch,
        compiler_params=pltpu.CompilerParams(
            collective_id=0, has_side_effects=True, vmem_limit_bytes=58 * 2**20
        ),
        name="sage",
    )(
        features,
        degrees.reshape(1, T),
        tile_values.reshape(128, T, T),
        tile_index.reshape(16, 8).T,
        tile_count.reshape(1, 16),
        self_weight,
        neigh_weight,
        bias.reshape(1, W),
        out_grad,
    )
    output, grad_features, self_grad, neigh_grad, bias_grad = pl.pallas_call(
        finish,
        out_shape=shapes,
        in_specs=[pl.BlockSpec(memory_space=pltpu.VMEM)] * 5,
        out_specs=[anywhere] * 5,
        scratch_shapes=[dma((5,))],
        compiler_params=pltpu.CompilerParams(vmem_limit_bytes=62 * 2**20),
        name="finish",
    )(*raw)
    return output, grad_features, self_grad, neigh_grad, bias_grad.reshape(W)


def solution(mesh):
    placed = (
        P(("row", "col"), None),
        P(("row", "col")),
        P("row", "col", None, None, None, None),
        P("row", "col", None, None),
        P("row", "col", None),
        P(),
        P(),
        P(),
        P(("row", "col"), None),
    )
    return jax.shard_map(
        local,
        mesh=mesh,
        in_specs=placed,
        out_specs=(P(("row", "col"), None), P(("row", "col"), None), P(), P(), P()),
        check_vma=False,
    )
```

```python
import functools

import jax
import jax.numpy as jnp
from jax import lax
from jax.experimental import pallas as pl
from jax.experimental.pallas import tpu as pltpu
from jax.sharding import PartitionSpec as P

MESH = pl.DeviceIdType.MESH
F32 = jnp.float32
BF16 = jnp.bfloat16
T = 128
W = 256
CHIPS = [(dx, dz) for dx in (2, 1, 3, 0) for dz in (1, 0) if dx or dz]
PLANE = [(dx, dy) for dx in range(4) for dy in range(4) if dx or dy]
FAR = (1, 3, 2)
FAR_FIRST = (2, 1, 3, 0)
GELU_C = 0.7978845608028654


def dot(lhs, rhs, lhs_dim=1, rhs_dim=0):
    return lax.dot_general(
        lhs, rhs, (((lhs_dim,), (rhs_dim,)), ((), ())), preferred_element_type=F32
    )


def device(x, zl, c, y, zh):
    return (x * 4 + zl * 2 + c, y * 4 + zh)


def piece_at(x, zl, c):
    return c * 8 + x * 2 + zl


def split_rows(total):
    high = total.astype(BF16).astype(F32)
    return high, total - high


def bias_block(total):
    high, low = split_rows(total)
    line = lax.broadcasted_iota(jnp.int32, (16, W), 0)
    return jnp.where(line == 0, high, jnp.where(line == 1, low, 0.0)).astype(BF16)


def kernel(
    feats_h, deg_h, tiles_h, index_h, count_h, ws_h, wn_h, bias_h, og_h,
    out_h, gf_h, sg_h, ng_h, bg_h,
    out_v, gf_v, ar4, ar5_r, sg_v, ng_v, bg_v, tiles, dense, index_v, count_v, slot_v, slot_s, feats_all, grads_all,
    deg_v, ws, wn, bias_v, og_v, base, recip, sums, part_b, recv_by, sum_z, recv_bz, self_keep,
    part_d, keep_d, recv_ds, sum_d, recv_d, ar1_s, ar1_r, ar2_s, ar2_r, ar3_s, ar3_r,
    local_sem, a_ss, a_rs, af_ss, af_rs, by_ss, by_rs, bz_ss, bz_rs,
    cz_ss, cz_rs, cy_ss, cy_rs, ds_ss, ds_rs, d_ss, d_rs,
    r1_ss, r1_rs, r2_ss, r2_rs, r3_ss, r3_rs, r4_ss, r4_rs, r5_ss, r5_rs,
):
    a = lax.axis_index("row")
    b = lax.axis_index("col")
    x, zl, c = a // 4, (a // 2) % 2, a % 2
    y, zh = b // 4, b % 4
    z = zh * 2 + zl
    sib = device(x, zl, 1 - c, y, zh)
    home = piece_at(x, zl, c)
    sent = []

    def send(src, dst, send_sem, recv_sem, where):
        copy = pltpu.make_async_remote_copy(
            src_ref=src, dst_ref=dst, send_sem=send_sem, recv_sem=recv_sem,
            device_id=where, device_id_type=MESH,
        )
        copy.start()
        sent.append(copy)
        return copy

    def chip(dx, dz):
        return (x + dx) % 4, (zl + dz) % 2

    partners = [sib]
    partners += [device(*chip(dx, dz), c, y, zh) for dx, dz in CHIPS]
    partners += [device((x + dx) % 4, zl, c, (y + dy) % 4, zh) for dx, dy in PLANE if dy]
    partners += [
        device(x, zz % 2, c, y, zz // 2)
        for zz in [(z + d) % 8 for d in range(1, 8)]
    ]
    barrier = pltpu.get_barrier_semaphore()
    for partner in reversed(partners):
        pl.semaphore_signal(barrier, inc=1, device_id=partner, device_id_type=MESH)

    halves = [feats_h.at[:, pl.ds(h * T, T)] for h in range(2)]
    small = [
        pltpu.make_async_copy(index_h, index_v, local_sem.at[2]),
        pltpu.make_async_copy(count_h, count_v, local_sem.at[3]),
    ]
    large = [
        pltpu.make_async_copy(tiles_h, tiles, local_sem.at[9]),
        pltpu.make_async_copy(ws_h, ws, local_sem.at[4]),
        pltpu.make_async_copy(wn_h, wn, local_sem.at[5]),
        pltpu.make_async_copy(bias_h, bias_v, local_sem.at[6]),
        pltpu.make_async_copy(og_h, og_v, local_sem.at[7]),
        pltpu.make_async_copy(deg_h, deg_v, local_sem.at[8]),
    ]
    large += [
        pltpu.make_async_copy(halves[h], feats_all.at[h, home], local_sem.at[h])
        for h in range(2)
    ]
    for load in small + large:
        load.start()
    pl.semaphore_wait(barrier, len(partners))

    a_sent = []

    def send_half(h):
        there = feats_all.at[h, home]
        a_sent.append(
            [
                send(
                    halves[h], there, a_ss.at[h, j], a_rs.at[h, j],
                    device(*chip(dx, dz), c, y, zh),
                )
                for j, (dx, dz) in enumerate(CHIPS)
            ]
            + [send(halves[h], there, a_ss.at[h, 7], a_rs.at[h, 7], sib)]
        )

    send_half(0)

    for load in small:
        load.wait()
    place = lax.broadcasted_iota(jnp.int32, (16, 16), 0)
    slot = jnp.full((16, 16), 8, jnp.int32)
    for k in range(8):
        here = (index_v[k : k + 1] == place) & (count_v[...] > k)
        slot = jnp.where(here, k, slot)
    slot_v[:, 0:16] = slot
    to_scalar = pltpu.make_async_copy(slot_v, slot_s, local_sem.at[10])
    to_scalar.start()
    to_scalar.wait()
    for load in large:
        load.wait()

    def build(q, carry):
        r = (q % 4) * 4 + q // 4
        for p in range(16):
            at = piece_at(p // 4, (p // 2) % 2, p % 2)
            slot = slot_s[r, p]
            tile = tiles[p * 8 + jnp.minimum(slot, 7)]
            dense[q, :, at * T : (at + 1) * T] = jnp.where(
                slot < 8, tile, jnp.zeros_like(tile)
            )
        return carry

    lax.fori_loop(0, 16, build, 0)
    send_half(1)
    feats = jnp.concatenate([feats_all[0, home], feats_all[1, home]], axis=1)
    base[...] = dot(feats, ws[...]) + bias_v[...]
    inverse = jnp.broadcast_to(1.0 / deg_v[...].astype(F32), (T, T)).T
    recip[...] = inverse

    by_sent = []

    def shares(h, core, i):
        zz = (zh + FAR_FIRST[i]) % 4
        columns = pl.ds(pl.multiple_of(core * 8 * T, 8 * T), 8 * T)
        block = dense[pl.ds(zz * 4, 4), :, columns].reshape(4 * T, 8 * T)
        return dot(block, feats_all[h, pl.ds(core * 8, 8)].reshape(8 * T, T))

    for h in range(2):
        forwards = []
        for j in (6, 3, 5, 1, 2, 4, 0):
            dx, dz = CHIPS[j]
            a_sent[h][j].wait_recv()
            piece = feats_all.at[h, piece_at(*chip(-dx, dz), c)]
            forwards.append(send(piece, piece, af_ss.at[h, j], af_rs.at[h, j], sib))
        for i in range(4):
            sums[i] = shares(h, c, i)
        a_sent[h][7].wait_recv()
        for copy in forwards:
            copy.wait_recv()
        for i, dz in enumerate(FAR_FIRST):
            zz = (zh + dz) % 4
            part = sums[i] + shares(h, 1 - c, i)
            part_b[h, i] = part.reshape(4, T, T).astype(BF16)
            row = []
            for k, dy in enumerate(FAR):
                yy = (y + dy) % 4
                row.append(
                    send(
                        part_b.at[h, i, yy], recv_by.at[h, i, k],
                        by_ss.at[h, i, k], by_rs.at[h, i, k], device(x, zl, c, yy, zh),
                    )
                )
            by_sent.append(row)

    bz_sent = []
    owns = []
    for h in range(2):
        for i, dz in enumerate(FAR_FIRST):
            total = part_b[h, i, y].astype(F32)
            for k in range(3):
                by_sent[h * 4 + i][k].wait_recv()
                total = total + recv_by[h, i, k].astype(F32)
            if dz:
                sum_z[h, i] = total.astype(BF16)
                bz_sent.append(
                    send(
                        sum_z.at[h, i], recv_bz.at[h, i], bz_ss.at[h, i], bz_rs.at[h, i],
                        device(x, zl, c, y, (zh + dz) % 4),
                    )
                )
            else:
                owns.append(total)
    means = []
    pre = base[...]
    for h in range(2):
        total = owns[h]
        for i in range(3):
            bz_sent[h * 3 + i].wait_recv()
            total = total + recv_bz[h, i].astype(F32)
        means.append((total * recip[...]).astype(BF16))
        pre = pre + dot(means[h], wn[h * T : (h + 1) * T])

    tanh = jnp.tanh(GELU_C * (pre + 0.044715 * (pre * pre * pre)))
    slope = 0.5 * (1.0 + tanh) + 0.5 * pre * (1.0 - tanh * tanh) * (
        GELU_C * (1.0 + 3.0 * 0.044715 * (pre * pre))
    )
    gp = (og_v[...].astype(F32) * slope).astype(BF16)

    me = zh * 4 + y
    cz_sent = []
    cy_sent = [[], []]
    for h in range(2):
        mine = grads_all.at[h, me]
        grads_all[h, me] = (dot(gp, wn[h * T : (h + 1) * T], 1, 1) * recip[...]).astype(BF16)
        cz_sent.append(
            [
                send(
                    mine, mine, cz_ss.at[h, k], cz_rs.at[h, k],
                    device(x, zl, c, y, (zh + d) % 4),
                )
                for k, d in enumerate(FAR)
            ]
        )
        for k, d in enumerate(FAR):
            cy_sent[h].append(
                send(
                    mine, mine, cy_ss.at[h, 3, k], cy_rs.at[h, 3, k],
                    device(x, zl, c, (y + d) % 4, zh),
                )
            )

    out_v[...] = (0.5 * pre * (1.0 + tanh)).astype(BF16)
    stores = [pltpu.make_async_copy(out_v, out_h, local_sem.at[11])]
    stores[0].start()

    mean = jnp.concatenate(means, axis=1)
    feats = jnp.concatenate([feats_all[0, home], feats_all[1, home]], axis=1)
    self_part = dot(feats, gp, 0, 0)
    neigh_part = dot(mean, gp, 0, 0)
    bias_part = jnp.sum(gp.astype(F32), axis=0, keepdims=True)
    first = c == 0
    ar1_s[0:W] = jnp.where(first, neigh_part, self_part).astype(BF16)
    ar1_s[W : W + 16] = bias_block(bias_part)
    r1 = send(ar1_s, ar1_r, r1_ss, r1_rs, sib)
    keep = jnp.where(first, self_part, neigh_part)
    self_keep[...] = dot(gp, ws[...], 1, 1)
    r1.wait_recv()
    chunk = keep + ar1_r[0:W].astype(F32)
    ar2_s[:, 0:16] = chunk.reshape(16, 16, W).astype(BF16)
    other = ar1_r[W : W + 16].astype(F32)
    mine = ar1_s[W : W + 16].astype(F32)
    both = jnp.sum(mine + other, axis=0, keepdims=True)
    ar2_s[:, 16:32] = jnp.broadcast_to(bias_block(both)[None], (16, 16, W))
    def pass_along(h):
        for k in range(3):
            cz_sent[h][k].wait_recv()
            piece = grads_all.at[h, ((zh - FAR[k]) % 4) * 4 + y]
            for m, dy in enumerate(FAR):
                cy_sent[h].append(
                    send(
                        piece, piece, cy_ss.at[h, k, m], cy_rs.at[h, k, m],
                        device(x, zl, c, (y + dy) % 4, zh),
                    )
                )

    pass_along(0)
    spot = x * 4 + y
    r2 = []
    for j, (dx, dy) in enumerate(PLANE):
        xx, yy = (x + dx) % 4, (y + dy) % 4
        r2.append(
            send(
                ar2_s.at[xx * 4 + yy], ar2_r.at[spot], r2_ss.at[j], r2_rs.at[j],
                device(xx, zl, c, yy, zh),
            )
        )
    ar2_r[spot] = ar2_s[spot]
    pass_along(1)

    for copy in r2:
        copy.wait_recv()
    total = jnp.zeros((32, W), F32)
    for j in range(16):
        total = total + ar2_r[j].astype(F32)
    ar3_s[0:16] = total[0:16].astype(BF16)
    ar3_s[16:32] = bias_block(jnp.sum(total[16:32], axis=0, keepdims=True))
    r3 = []
    for j in range(7):
        zz = (z + j + 1) % 8
        r3.append(
            send(
                ar3_s, ar3_r.at[z], r3_ss.at[j], r3_rs.at[j], device(x, zz % 2, c, y, zz // 2)
            )
        )
    ar3_r[z] = ar3_s[...]

    ds_sent = []
    d_sent = [[], []]

    def half_terms(h, core, i):
        at = core * 8 + (x + FAR_FIRST[i]) % 4 * 2
        columns = pl.ds(pl.multiple_of(at * T, 2 * T), 2 * T)
        block = dense[:, :, columns].reshape(16 * T, 2 * T)
        return dot(block, grads_all[h].reshape(16 * T, T), 0, 0).reshape(2, T, T)

    def terms(h, i):
        part_d[h, i] = half_terms(h, 1 - c, i).astype(BF16)
        ds_sent.append(
            send(part_d.at[h, i], recv_ds.at[h, i], ds_ss.at[h, i], ds_rs.at[h, i], sib)
        )
        keep_d[h, i] = half_terms(h, c, i)

    def pass_on(h, i):
        dx = FAR_FIRST[i]
        ds_sent[h * 4 + i].wait_recv()
        total = keep_d[h, i] + recv_ds[h, i].astype(F32)
        sum_d[h, i] = total.astype(BF16)
        for dz in (1, 0):
            if dx or dz:
                xx, zz = chip(dx, dz)
                j = CHIPS.index((dx, dz))
                d_sent[h].append(
                    send(
                        sum_d.at[h, i, zz], recv_d.at[h, j], d_ss.at[h, j], d_rs.at[h, j],
                        device(xx, zz, c, y, zh),
                    )
                )

    for copy in cy_sent[0]:
        copy.wait_recv()
    for i in range(4):
        terms(0, i)
        if i:
            pass_on(0, i - 1)
    pass_on(0, 3)

    for copy in r3:
        copy.wait_recv()
    total = jnp.zeros((32, W), F32)
    for j in range(8):
        total = total + ar3_r[j].astype(F32)
    bg_v[...] = jnp.sum(total[16:32], axis=0, keepdims=True)
    ar4[spot] = total[0:16].astype(BF16)
    r4 = []
    for j, (dx, dy) in enumerate(PLANE):
        xx, yy = (x + dx) % 4, (y + dy) % 4
        r4.append(
            send(
                ar4.at[spot], ar4.at[spot], r4_ss.at[j], r4_rs.at[j], device(xx, zl, c, yy, zh)
            )
        )

    for copy in cy_sent[1]:
        copy.wait_recv()
    for i in range(4):
        terms(1, i)
        if i:
            pass_on(1, i - 1)
    pass_on(1, 3)

    for copy in r4:
        copy.wait_recv()
    r5 = send(ar4, ar5_r, r5_ss, r5_rs, sib)

    def total_back(h):
        back = self_keep[:, h * T : (h + 1) * T] + sum_d[h, 3, zl].astype(F32)
        for copy in d_sent[h]:
            copy.wait_recv()
        for j in range(7):
            back = back + recv_d[h, j].astype(F32)
        gf_v[:, h * T : (h + 1) * T] = back.astype(BF16)

    total_back(0)
    r5.wait_recv()
    here = ar4[...].reshape(W, W).astype(F32)
    there = ar5_r[...].reshape(W, W).astype(F32)
    sg_v[...] = jnp.where(first, here, there)
    ng_v[...] = jnp.where(first, there, here)
    stores += [
        pltpu.make_async_copy(sg_v, sg_h, local_sem.at[12]),
        pltpu.make_async_copy(ng_v, ng_h, local_sem.at[13]),
        pltpu.make_async_copy(bg_v, bg_h, local_sem.at[14]),
    ]
    for store in stores[1:]:
        store.start()
    for copy in sent:
        copy.wait_send()
    total_back(1)
    stores.append(pltpu.make_async_copy(gf_v, gf_h, local_sem.at[15]))
    stores[-1].start()
    for store in stores:
        store.wait()


def finish(*refs):
    stores = [
        pltpu.make_async_copy(refs[i], refs[5 + i], refs[10].at[i]) for i in range(5)
    ]
    for store in stores:
        store.start()
    for store in stores:
        store.wait()


def local(
    features, degrees, tile_values, tile_index, tile_count, self_weight, neigh_weight, bias,
    out_grad,
):
    vm = pltpu.VMEM
    dma = pltpu.SemaphoreType.DMA
    anywhere = pl.BlockSpec(memory_space=pl.ANY)
    scratch = [
        vm((T, W), BF16), vm((T, W), BF16), vm((16, 16, W), BF16), vm((16, 16, W), BF16),
        vm((W, W), F32), vm((W, W), F32), vm((1, W), F32),
        vm((128, T, T), BF16), vm((16, T, 16 * T), BF16),
        vm((8, 16), jnp.int32), vm((1, 16), jnp.int32), vm((16, T), jnp.int32),
        pltpu.SMEM((16, T), jnp.int32),
        vm((2, 16, T, T), BF16), vm((2, 16, T, T), BF16),
        vm((1, T), jnp.int32), vm((W, W), BF16), vm((W, W), BF16), vm((1, W), F32),
        vm((T, W), BF16),
        vm((T, W), F32), vm((T, T), F32),
        vm((4, 4 * T, T), F32),
        vm((2, 4, 4, T, T), BF16), vm((2, 4, 3, T, T), BF16), vm((2, 3, T, T), BF16),
        vm((2, 3, T, T), BF16), vm((T, W), F32),
        vm((2, 4, 2, T, T), BF16), vm((2, 4, 2, T, T), F32), vm((2, 4, 2, T, T), BF16), vm((2, 4, 2, T, T), BF16),
        vm((2, 7, T, T), BF16),
        vm((W + 16, W), BF16), vm((W + 16, W), BF16),
        vm((16, 32, W), BF16), vm((16, 32, W), BF16),
        vm((32, W), BF16), vm((8, 32, W), BF16),
        dma((16,)), dma((2, 8)), dma((2, 8)), dma((2, 7)), dma((2, 7)),
        dma((2, 4, 3)), dma((2, 4, 3)), dma((2, 3)), dma((2, 3)),
        dma((2, 3)), dma((2, 3)), dma((2, 4, 3)), dma((2, 4, 3)),
        dma((2, 4)), dma((2, 4)), dma((2, 7)), dma((2, 7)),
        dma(()), dma(()), dma((15,)), dma((15,)), dma((7,)), dma((7,)),
        dma((15,)), dma((15,)), dma(()), dma(()),
    ]
    shapes = (
        jax.ShapeDtypeStruct((T, W), BF16),
        jax.ShapeDtypeStruct((T, W), BF16),
        jax.ShapeDtypeStruct((W, W), F32),
        jax.ShapeDtypeStruct((W, W), F32),
        jax.ShapeDtypeStruct((1, W), F32),
    )
    raw = pl.pallas_call(
        kernel,
        out_shape=shapes,
        in_specs=[anywhere] * 9,
        out_specs=[anywhere] * 5,
        scratch_shapes=scratch,
        compiler_params=pltpu.CompilerParams(
            collective_id=0, has_side_effects=True, vmem_limit_bytes=58 * 2**20
        ),
        name="sage",
    )(
        features,
        degrees.reshape(1, T),
        tile_values.reshape(128, T, T),
        tile_index.reshape(16, 8).T,
        tile_count.reshape(1, 16),
        self_weight,
        neigh_weight,
        bias.reshape(1, W),
        out_grad,
    )
    output, grad_features, self_grad, neigh_grad, bias_grad = pl.pallas_call(
        finish,
        out_shape=shapes,
        in_specs=[pl.BlockSpec(memory_space=pltpu.VMEM)] * 5,
        out_specs=[anywhere] * 5,
        scratch_shapes=[dma((5,))],
        compiler_params=pltpu.CompilerParams(vmem_limit_bytes=62 * 2**20),
        name="finish",
    )(*raw)
    return output, grad_features, self_grad, neigh_grad, bias_grad.reshape(W)


def solution(mesh):
    placed = (
        P(("row", "col"), None),
        P(("row", "col")),
        P("row", "col", None, None, None, None),
        P("row", "col", None, None),
        P("row", "col", None),
        P(),
        P(),
        P(),
        P(("row", "col"), None),
    )
    return jax.shard_map(
        local,
        mesh=mesh,
        in_specs=placed,
        out_specs=(P(("row", "col"), None), P(("row", "col"), None), P(), P(), P()),
        check_vma=False,
    )
```
